512 devices in a mesh: group: 32 (over x_hi, y, core), member: 16 (over x_lo, z).
Axes of the slice: x: 4 (x_hi: 2, x_lo: 2; x = x_hi * 2 + x_lo), y: 8, z: 8, core: 2. Of those that a mesh axis runs over, the one named last changes fastest.
Arguments:
- images: bfloat16 [16384, 1152], P(('group', 'member')), may hold values from -1.1953125 to 1.1953125
- texts: bfloat16 [16384, 1152], P(('group', 'member')), may hold values from -1.1953125 to 1.1953125
Outputs:
- image_grad: float32 [16384, 1152], P(('group', 'member'))
- text_grad: float32 [16384, 1152], P(('group', 'member'))
The draws below stay inside these ranges and needn't reach their ends.
All inputs are finite; a program needn't handle non-finite values.
Results may differ from the reference program's by a relative error of at most 0.039.
Values may be sent and summed in bfloat16 or wider, within the bound.
No kernel may reach another device: no remote copies, remote signals or barrier semaphores. Data moves between devices by JAX's collectives and lax.ppermute only.
A program may use at most 64 MiB of HBM per device.

```python
import jax
import jax.numpy as jnp
from jax import lax

D = 1152
ROWS_DEV = 32
BATCH = 16384
N_GROUP = 32
N_MEMBER = 16


def level_of(key, shape, pieces, smallest, top_value):
    gain, own = 1.0, jax.random.fold_in(key, 6)
    for axis_at, parts in pieces:
        steps = jnp.exp(jax.random.uniform(jax.random.fold_in(own, axis_at), (parts,), jnp.float32, smallest / len(pieces), top_value / len(pieces)))
        gain = gain * jnp.repeat(steps, shape[axis_at] // parts).reshape([-1 if axis == axis_at else 1 for axis in range(len(shape))])
    return gain


def scatter_about(key, dims, spread, most, shards=(), held_as=jnp.bfloat16):
    drawn = spread * jax.random.normal(key, dims, jnp.float32)
    if shards:
        drawn = drawn * level_of(key, dims, shards, -0.22, 0.18)
    return jnp.clip(drawn, -most, most).astype(held_as)


def setup_inputs(seed: int = 0) -> dict:
    key_of = jax.random.split(jax.random.key(seed), 3)
    images = scatter_about(key_of[0], (BATCH, D), 0.2, 1.1953125, ((0, 512),))
    texts = scatter_about(key_of[1], (BATCH, D), 0.2, 1.1953125, ((0, 512),))
    return {"images": images, "texts": texts}


logit_scale = 30.0
logit_bias = -5.0
epsilon = 1e-06

def unit_rows(raw):
    wide = raw.astype(jnp.float32)
    inverse = lax.rsqrt(lax.optimization_barrier(jnp.sum(wide * wide, axis=1, keepdims=True)) + epsilon)
    return (wide * inverse, inverse)

def tile_coef(img_block, txt_block, start, group_idx, member_idx, rows):
    scores = jnp.dot(img_block, txt_block.T, preferred_element_type=jnp.float32)
    logits = logit_scale * scores + logit_bias
    img_pos = jnp.arange(img_block.shape[0], dtype=jnp.int32)[:, None]
    txt_pos = start + jnp.arange(txt_block.shape[0], dtype=jnp.int32)[None, :]
    same = (txt_pos // rows == group_idx) & (img_pos // rows == member_idx) & (txt_pos % rows == img_pos % rows)
    label = same.astype(jnp.float32)
    return (logit_scale * (jax.nn.sigmoid(logits) - label)).astype(jnp.bfloat16)

def raw_grad(unit_sum, unit, inverse):
    along = lax.optimization_barrier(jnp.sum(unit_sum * unit, axis=1, keepdims=True))
    return inverse * (unit_sum - along * unit)

def reference(images, texts):
    rows = ROWS_DEV
    img_unit, img_inv = unit_rows(images)
    txt_unit, txt_inv = unit_rows(texts)
    img_bf = img_unit.astype(jnp.bfloat16)
    txt_bf = txt_unit.astype(jnp.bfloat16)
    txt_cols = txt_bf.reshape(N_GROUP, N_MEMBER, rows, D).transpose(1, 0, 2, 3).reshape(N_MEMBER, N_GROUP * rows, D)
    members = jnp.arange(N_MEMBER, dtype=jnp.int32)

    def one_group(carry, group_idx):
        img_block = lax.dynamic_slice_in_dim(img_bf, group_idx * (N_MEMBER * rows), N_MEMBER * rows, 0)

        def one_tile(txt_block, member_idx):
            coef = tile_coef(img_block, txt_block, jnp.int32(0), group_idx, member_idx, rows)
            img_part = jnp.dot(coef, txt_block, preferred_element_type=jnp.float32).astype(jnp.bfloat16)
            txt_part = jnp.dot(coef.T, img_block, preferred_element_type=jnp.float32).astype(jnp.bfloat16)
            return (img_part, txt_part)
        img_parts, txt_parts = jax.vmap(one_tile)(txt_cols, members)
        img_parts = lax.optimization_barrier(img_parts)
        txt_parts = lax.optimization_barrier(txt_parts)
        img_sum = lax.optimization_barrier(jnp.sum(img_parts.astype(jnp.float32), axis=0))
        return (carry + txt_parts.astype(jnp.float32), img_sum)
    start_acc = jnp.zeros((N_MEMBER, N_GROUP * rows, D), jnp.float32)
    txt_acc, img_sums = lax.scan(one_group, start_acc, jnp.arange(N_GROUP, dtype=jnp.int32))
    img_sum = img_sums.reshape(N_GROUP * N_MEMBER * rows, D)
    txt_sum = txt_acc.reshape(N_MEMBER, N_GROUP, rows, D).transpose(1, 0, 2, 3).reshape(N_GROUP * N_MEMBER * rows, D)
    return (raw_grad(img_sum, img_unit, img_inv), raw_grad(txt_sum, txt_unit, txt_inv))
```

```python
import jax
import jax.numpy as jnp
from jax import lax
from jax.sharding import Mesh, PartitionSpec as P

logit_scale = 30.0
logit_bias = -5.0
epsilon = 1e-06

AXES = ("xh", "y", "core", "xl", "z")
SIZES = (2, 8, 2, 2, 8)
ALL = P(AXES, None)
SWAP = [(0, 1), (1, 0)]


def index_of(xh, y, core, xl, z):
    return (((xh * 8 + y) * 2 + core) * 2 + xl) * 8 + z


def line_groups():
    groups = []
    for xh in range(2):
        for y in range(8):
            groups.append([index_of(xh, y, 0, xl, z) for xl in range(2) for z in range(8)])
    for pair in range(2):
        for z in range(8):
            groups.append([index_of(xh, y, 1, xh ^ pair, z) for xh in range(2) for y in range(8)])
    return groups


def unit_rows(raw):
    wide = raw.astype(jnp.float32)
    inverse = lax.rsqrt(jnp.sum(wide * wide, axis=1, keepdims=True) + epsilon)
    return (wide * inverse, inverse)


def raw_grad(unit_sum, unit, inverse):
    along = jnp.sum(unit_sum * unit, axis=1, keepdims=True)
    return inverse * (unit_sum - along * unit)


def exchange(blocks, groups):
    return lax.all_to_all(
        blocks, AXES, split_axis=0, concat_axis=0, axis_index_groups=groups, tiled=True
    )


def local(images, texts):
    rows, width = images.shape
    half, full = 16 * rows, 32 * rows
    xh, y, core, xl, z = (lax.axis_index(name) for name in AXES)
    first = core == 0
    groups = line_groups()

    own = jnp.where(first, images, texts)
    other = lax.ppermute(jnp.where(first, texts, images), "core", SWAP)
    pair = jnp.where(
        first, jnp.concatenate([own, other], 0), jnp.concatenate([other, own], 0)
    )
    unit, inverse = unit_rows(pair)
    unit_bf = unit.astype(jnp.bfloat16)
    line = exchange(jnp.concatenate([unit_bf] * 16, 0), groups)

    near = lax.ppermute(line[:half], "core", SWAP)
    far = lax.ppermute(line[half:], "core", [(0, 1)])
    img = jnp.where(first, line, jnp.concatenate([near, far], 0))
    txt = jnp.where(first, near, line[half:])

    scores = jnp.dot(img, txt.T, preferred_element_type=jnp.float32)
    logits = logit_scale * scores + logit_bias
    img_pos = jnp.arange(full, dtype=jnp.int32)[:, None] - (xl * 8 + z) * (2 * rows)
    txt_pos = (
        jnp.arange(half, dtype=jnp.int32)[None, :] + core * half - (xh * 8 + y) * (2 * rows)
    )
    same = (img_pos == txt_pos) & (img_pos >= 0) & (img_pos < 2 * rows)
    label = same.astype(jnp.float32)
    coef = (logit_scale * (jax.nn.sigmoid(logits) - label)).astype(jnp.bfloat16)

    img_part = jnp.dot(coef, txt, preferred_element_type=jnp.float32)
    txt_part = lax.dot_general(
        coef, img, (((0,), (0,)), ((), ())), preferred_element_type=jnp.float32
    )
    img_bf = img_part.astype(jnp.bfloat16)
    txt_bf = txt_part.astype(jnp.bfloat16)
    near = lax.ppermute(jnp.where(first, txt_bf, img_bf[:half]), "core", SWAP)
    far = lax.ppermute(img_bf[half:], "core", [(1, 0)])
    img_all = jnp.concatenate([near, far], 0).astype(jnp.float32) + img_part
    txt_all = jnp.concatenate([near, txt_bf], 0)
    parts = exchange(jnp.where(first, img_all.astype(jnp.bfloat16), txt_all), groups)
    total = jnp.sum(parts.reshape(16, 2 * rows, width).astype(jnp.float32), axis=0)
    grad = raw_grad(total, unit, inverse)
    kept = jnp.where(first, grad[:rows], grad[rows:])
    got = lax.ppermute(jnp.where(first, grad[rows:], grad[:rows]), "core", SWAP)
    return (jnp.where(first, kept, got), jnp.where(first, got, kept))


def solution(mesh):
    fine = Mesh(mesh.devices.reshape(SIZES), AXES)
    return jax.shard_map(
        local, mesh=fine, in_specs=(ALL, ALL), out_specs=(ALL, ALL), check_vma=False
    )
```

```python
import jax
import jax.numpy as jnp
from jax import lax
from jax.sharding import Mesh, PartitionSpec as P

logit_scale = 30.0
logit_bias = -5.0
epsilon = 1e-06

AXES = ("xh", "y", "core", "xl", "z")
SIZES = (2, 8, 2, 2, 8)
ALL = P(AXES, None)
SWAP = [(0, 1), (1, 0)]


def index_of(xh, y, core, xl, z):
    return (((xh * 8 + y) * 2 + core) * 2 + xl) * 8 + z


def devices():
    for xh in range(2):
        for y in range(8):
            for core in range(2):
                for xl in range(2):
                    for z in range(8):
                        yield xh, y, core, xl, z


def line_step(step):
    pairs = []
    for xh, y, core, xl, z in devices():
        to = (xh, y, core, xl, (z + step) % 8) if core == 0 else (xh, (y + step) % 8, core, xl, z)
        pairs.append((index_of(xh, y, core, xl, z), index_of(*to)))
    return pairs


def across_x():
    pairs = []
    for xh, y, core, xl, z in devices():
        to = (xh ^ core, y, core, 1 - xl, z)
        pairs.append((index_of(xh, y, core, xl, z), index_of(*to)))
    return pairs


def send(block, pairs):
    return lax.ppermute(block, AXES, pairs)


def unit_rows(raw):
    wide = raw.astype(jnp.float32)
    inverse = lax.rsqrt(jnp.sum(wide * wide, axis=1, keepdims=True) + epsilon)
    return (wide * inverse, inverse)


def raw_grad(unit_sum, unit, inverse):
    along = jnp.sum(unit_sum * unit, axis=1, keepdims=True)
    return inverse * (unit_sum - along * unit)


def pull(mine, theirs, own_pairs):
    scores = lax.dot_general(
        mine, theirs, (((1,), (1,)), ((), ())), preferred_element_type=jnp.float32
    )
    chance = jax.nn.sigmoid(logit_scale * scores + logit_bias)
    if own_pairs:
        row = lax.broadcasted_iota(jnp.int32, chance.shape, 0)
        column = lax.broadcasted_iota(jnp.int32, chance.shape, 1)
        chance = chance - ((row == column) & (row < own_pairs)).astype(jnp.float32)
    coef = (logit_scale * chance).astype(jnp.bfloat16)
    return jnp.dot(coef, theirs, preferred_element_type=jnp.float32)


def local(images, texts):
    rows, width = images.shape
    chip = 2 * rows
    first = lax.axis_index("core") == 0
    bf = jnp.bfloat16

    own = jnp.where(first, images, texts)
    other = lax.ppermute(jnp.where(first, texts, images), "core", SWAP)
    pair = jnp.where(
        first, jnp.concatenate([own, other], 0), jnp.concatenate([other, own], 0)
    )
    unit, inverse = unit_rows(pair)
    unit_bf = unit.astype(bf)

    up3 = send(unit_bf, line_step(-3))
    down3 = send(unit_bf, line_step(3))
    three = jnp.concatenate([unit_bf, up3, down3], 0)
    far_three = send(three, across_x())
    up1 = send(three, line_step(-1))
    down1 = send(three[: 2 * chip], line_step(1))
    five = jnp.concatenate([up1, down1], 0)
    far_five = send(five, across_x())

    mine = jnp.concatenate([three, five, far_three], 0)
    theirs = lax.ppermute(mine, "core", SWAP)
    their_five = lax.ppermute(far_five, "core", SWAP)

    near_sum = pull(mine, theirs, chip)
    far_sum = pull(far_five, theirs, 0) + pull(far_five, their_five, 0)
    back_five = send(far_sum.astype(bf), across_x())
    near_sum = near_sum + pull(mine, their_five, 0)
    back_three = send(near_sum[8 * chip :].astype(bf), across_x())

    sum_five = (near_sum[3 * chip : 8 * chip] + back_five.astype(jnp.float32)).astype(bf)
    from_down = send(sum_five[: 3 * chip], line_step(1)).astype(jnp.float32)
    from_up = send(sum_five[3 * chip :], line_step(-1)).astype(jnp.float32)
    sum_three = near_sum[: 3 * chip] + back_three.astype(jnp.float32) + from_down
    sum_two = sum_three[: 2 * chip] + from_up
    from_down = send(sum_two[chip:].astype(bf), line_step(3))
    from_up = send(sum_three[2 * chip :].astype(bf), line_step(-3))
    total = sum_two[:chip] + from_down.astype(jnp.float32) + from_up.astype(jnp.float32)

    grad = raw_grad(total, unit, inverse)
    kept = jnp.where(first, grad[:rows], grad[rows:])
    got = lax.ppermute(jnp.where(first, grad[rows:], grad[:rows]), "core", SWAP)
    return (jnp.where(first, kept, got), jnp.where(first, got, kept))


def solution(mesh):
    fine = Mesh(mesh.devices.reshape(SIZES), AXES)
    return jax.shard_map(
        local, mesh=fine, in_specs=(ALL, ALL), out_specs=(ALL, ALL), check_vma=False
    )
```

```python
import jax
import jax.numpy as jnp
from jax import lax
from jax.experimental import pallas as pl
from jax.experimental.pallas import tpu as pltpu
from jax.sharding import Mesh, PartitionSpec as P

logit_scale = 30.0
logit_bias = -5.0
epsilon = 1e-06

AXES = ("xh", "y", "core", "xl", "z")
SIZES = (2, 8, 2, 2, 8)
ALL = P(AXES, None)
SWAP = [(0, 1), (1, 0)]
LINE = 8


def index_of(xh, y, core, xl, z):
    return (((xh * 8 + y) * 2 + core) * 2 + xl) * 8 + z


def line_groups():
    groups = []
    for xh in range(2):
        for xl in range(2):
            for at in range(8):
                groups.append([index_of(xh, at, 0, xl, z) for z in range(8)])
                groups.append([index_of(xh, y, 1, xl, at) for y in range(8)])
    return groups


def across_x():
    pairs = []
    for xh in range(2):
        for y in range(8):
            for core in range(2):
                for xl in range(2):
                    for z in range(8):
                        pairs.append(
                            (index_of(xh, y, core, xl, z), index_of(xh ^ core, y, core, 1 - xl, z))
                        )
    return pairs


def unit_rows(raw):
    wide = raw.astype(jnp.float32)
    inverse = lax.rsqrt(jnp.sum(wide * wide, axis=1, keepdims=True) + epsilon)
    return (wide * inverse, inverse)


def raw_grad(unit_sum, unit, inverse):
    along = jnp.sum(unit_sum * unit, axis=1, keepdims=True)
    return inverse * (unit_sum - along * unit)


def pull_kernel(labelled, added, *refs):
    refs = list(refs)
    at_ref = refs.pop(0) if labelled else None
    mine_ref, theirs_ref = refs[0], refs[1]
    out_ref = refs[-1]
    scores = lax.dot_general(
        mine_ref[...],
        theirs_ref[...],
        (((1,), (1,)), ((), ())),
        preferred_element_type=jnp.float32,
    )
    chance = 1.0 / (1.0 + jnp.exp(-logit_bias - logit_scale * scores))
    if labelled:
        block = scores.shape[0]
        row = lax.broadcasted_iota(jnp.int32, scores.shape, 0) + (
            pl.program_id(0) * block - at_ref[0]
        )
        column = lax.broadcasted_iota(jnp.int32, scores.shape, 1) - at_ref[1]
        same = (row == column) & (row >= 0) & (row < at_ref[2])
        chance = chance - same.astype(jnp.float32)
    coef = (logit_scale * chance).astype(jnp.bfloat16)
    terms = jnp.dot(coef, theirs_ref[...], preferred_element_type=jnp.float32)
    if added:
        terms = terms + refs[2][...]
    out_ref[...] = terms.astype(out_ref.dtype)


def pull(mine, theirs, at=None, so_far=None, dtype=jnp.float32, block=256):
    rows, width = mine.shape
    block_spec = pl.BlockSpec((block, width), lambda i: (i, 0))
    whole_spec = pl.BlockSpec(theirs.shape, lambda i: (0, 0))
    args, specs = [mine, theirs], [block_spec, whole_spec]
    if at is not None:
        args.insert(0, at)
        specs.insert(0, pl.BlockSpec(memory_space=pltpu.SMEM))
    if so_far is not None:
        args.append(so_far)
        specs.append(block_spec)

    def kernel(*refs):
        pull_kernel(at is not None, so_far is not None, *refs)

    pairs = rows * theirs.shape[0]
    return pl.pallas_call(
        kernel,
        out_shape=jax.ShapeDtypeStruct((rows, width), dtype),
        grid=(rows // block,),
        in_specs=specs,
        out_specs=block_spec,
        compiler_params=pltpu.CompilerParams(vmem_limit_bytes=32 * 2**20),
        cost_estimate=pl.CostEstimate(
            flops=4 * pairs * width, bytes_accessed=8 * rows * width, transcendentals=2 * pairs
        ),
    )(*args)


def local(images, texts):
    rows, width = images.shape
    line = LINE * rows
    f32, bf = jnp.float32, jnp.bfloat16
    core = lax.axis_index("core")
    first = core == 0
    y, z = lax.axis_index("y"), lax.axis_index("z")
    my_place, their_place = jnp.where(first, z, y), jnp.where(first, y, z)
    groups, partners = line_groups(), across_x()

    def trade(blocks):
        return lax.all_to_all(
            blocks, AXES, split_axis=0, concat_axis=0, axis_index_groups=groups, tiled=True
        )

    def copies(block):
        return jnp.broadcast_to(block[None], (LINE, *block.shape)).reshape(-1, width)

    def swap_x(block):
        return lax.ppermute(block, AXES, partners)

    def swap_core(block):
        return lax.ppermute(block, "core", SWAP)

    def line_sum(blocks, size):
        return jnp.sum(blocks.reshape(LINE, size, width).astype(f32), axis=0)

    unit_a, inverse_a = unit_rows(jnp.where(first, images, texts))
    rows_a = unit_a.astype(bf)
    line_a = trade(copies(rows_a))
    unit_b, inverse_b = unit_rows(swap_core(jnp.where(first, texts, images)))
    rows_b = unit_b.astype(bf)
    both_b = jnp.concatenate([rows_b, swap_x(rows_b)], 0)

    mine_b = trade(copies(both_b))
    mine_a = jnp.concatenate([line_a, swap_x(line_a)], 0)
    theirs_a = swap_core(mine_a)
    sum_a = pull(mine_a, theirs_a)

    at_ab = jnp.stack([my_place * rows, their_place * 2 * rows, rows]).astype(jnp.int32)
    at_ba = jnp.stack([my_place * 2 * rows, their_place * rows, rows]).astype(jnp.int32)
    theirs_b = swap_core(mine_b)
    sum_b = pull(mine_b, theirs_a, at=at_ba)
    sum_b = pull(mine_b, theirs_b, so_far=sum_b, dtype=bf)

    back_b = trade(sum_b)
    sum_a = pull(mine_a, theirs_b, at=at_ab, so_far=sum_a)
    back_x = swap_x(sum_a[line:].astype(bf))
    back_a = trade((sum_a[:line] + back_x.astype(f32)).astype(bf))

    total_b = line_sum(back_b, 2 * rows)
    total_b = total_b[:rows] + swap_x(total_b[rows:].astype(bf)).astype(f32)
    got = swap_core(raw_grad(total_b, unit_b, inverse_b))
    kept = raw_grad(line_sum(back_a, rows), unit_a, inverse_a)
    return (jnp.where(first, kept, got), jnp.where(first, got, kept))


def solution(mesh):
    fine = Mesh(mesh.devices.reshape(SIZES), AXES)
    return jax.shard_map(
        local, mesh=fine, in_specs=(ALL, ALL), out_specs=(ALL, ALL), check_vma=False
    )
```

```python
import functools

import jax
import jax.numpy as jnp
from jax import lax
from jax.experimental import pallas as pl
from jax.experimental.pallas import tpu as pltpu
from jax.sharding import Mesh, PartitionSpec as P

logit_scale = 30.0
logit_bias = -5.0
epsilon = 1e-06

AXES = ("xh", "y", "core", "xl", "z")
SIZES = (2, 8, 2, 2, 8)
ALL = P(AXES, None)
SWAP = [(0, 1), (1, 0)]
LINE = 8

IN_VMEM = pl.BlockSpec(memory_space=pltpu.VMEM)
IN_HBM = pl.BlockSpec(memory_space=pltpu.HBM)
IN_SMEM = pl.BlockSpec(memory_space=pltpu.SMEM)
PARAMS = pltpu.CompilerParams(vmem_limit_bytes=16 * 2**20)


def index_of(xh, y, core, xl, z):
    return (((xh * 8 + y) * 2 + core) * 2 + xl) * 8 + z


def line_groups():
    groups = []
    for xh in range(2):
        for xl in range(2):
            for at in range(8):
                groups.append([index_of(xh, at, 0, xl, z) for z in range(8)])
                groups.append([index_of(xh, y, 1, xl, at) for y in range(8)])
    return groups


def across_x(role, core_to):
    pairs = []
    for xh in range(2):
        for y in range(8):
            for core in range(2):
                for xl in range(2):
                    for z in range(8):
                        to = (xh ^ role(core), y, core_to(core), 1 - xl, z)
                        pairs.append((index_of(xh, y, core, xl, z), index_of(*to)))
    return pairs


def unit_rows(raw):
    wide = raw.astype(jnp.float32)
    inverse = lax.rsqrt(jnp.sum(wide * wide, axis=1, keepdims=True) + epsilon)
    return (wide * inverse, inverse)


def raw_grad(unit_sum, raw):
    unit, inverse = unit_rows(raw)
    along = jnp.sum(unit_sum * unit, axis=1, keepdims=True)
    return inverse * (unit_sum - along * unit)


def fill(sources, out_ref, sems):
    copies, at = [], 0
    for _ in range(LINE):
        for source in sources:
            target = out_ref.at[pl.ds(at, source.shape[0])]
            copies.append(pltpu.make_async_copy(source, target, sems.at[len(copies)]))
            at += source.shape[0]
    for copy in copies:
        copy.start()
    for copy in copies:
        copy.wait()


def open_kernel(
    core_ref, images_hbm, texts_hbm, copies_ref, other_ref, images_ref, texts_ref, unit_ref, sems
):
    first = core_ref[0] == 0
    loads = [
        pltpu.make_async_copy(images_hbm, images_ref, sems.at[0]),
        pltpu.make_async_copy(texts_hbm, texts_ref, sems.at[1]),
    ]
    for load in loads:
        load.start()
    for load in loads:
        load.wait()
    img = unit_rows(images_ref[...])[0].astype(jnp.bfloat16)
    txt = unit_rows(texts_ref[...])[0].astype(jnp.bfloat16)
    unit_ref[...] = jnp.where(first, img, txt)
    other_ref[...] = jnp.where(first, txt, img)
    fill([unit_ref], copies_ref, sems)


def open_rows(core, images, texts):
    rows, width = images.shape
    return pl.pallas_call(
        open_kernel,
        out_shape=(
            jax.ShapeDtypeStruct((LINE * rows, width), jnp.bfloat16),
            jax.ShapeDtypeStruct((rows, width), jnp.bfloat16),
        ),
        in_specs=[IN_SMEM, IN_HBM, IN_HBM],
        out_specs=(IN_HBM, IN_VMEM),
        scratch_shapes=[pltpu.VMEM((rows, width), jnp.bfloat16)] * 3
        + [pltpu.SemaphoreType.DMA((LINE,))],
        compiler_params=PARAMS,
    )(core, images, texts)


def copies_kernel(one_ref, two_ref, out_ref, sems):
    fill([one_ref, two_ref], out_ref, sems)


def copies(one, two):
    rows, width = one.shape
    return pl.pallas_call(
        copies_kernel,
        out_shape=jax.ShapeDtypeStruct((2 * LINE * rows, width), one.dtype),
        in_specs=[IN_VMEM, IN_VMEM],
        out_specs=IN_HBM,
        scratch_shapes=[pltpu.SemaphoreType.DMA((2 * LINE,))],
        compiler_params=PARAMS,
    )(one, two)


def pull_kernel(parts, labelled, added, *refs):
    refs = list(refs)
    at_ref = refs.pop(0) if labelled else None
    mine_ref = refs.pop(0)
    terms = None
    for part in range(parts):
        theirs_ref = refs.pop(0)
        scores = lax.dot_general(
            mine_ref[...],
            theirs_ref[...],
            (((1,), (1,)), ((), ())),
            preferred_element_type=jnp.float32,
        )
        chance = 1.0 / (1.0 + jnp.exp(-logit_bias - logit_scale * scores))
        if labelled and part == parts - 1:
            row = lax.broadcasted_iota(jnp.int32, scores.shape, 0) - at_ref[0]
            column = lax.broadcasted_iota(jnp.int32, scores.shape, 1) - at_ref[1]
            same = (row == column) & (row >= 0) & (row < at_ref[2])
            chance = jnp.where(same, chance - 1.0, chance)
        coef = (logit_scale * chance).astype(jnp.bfloat16)
        if part < parts - 1:
            new = jnp.dot(coef, theirs_ref[...], preferred_element_type=jnp.float32)
            terms = new if terms is None else terms + new
    so_far_ref = refs.pop(0) if added else None
    out_ref = refs.pop(0)
    stores = []
    blocks = 2 if refs else 1
    size = mine_ref.shape[0] // blocks
    for block in range(blocks):
        rows = slice(block * size, (block + 1) * size)
        total = jnp.dot(coef[rows], theirs_ref[...], preferred_element_type=jnp.float32)
        if terms is not None:
            total = total + terms[rows]
        if added:
            total = total + so_far_ref[rows].astype(jnp.float32)
        if not refs:
            out_ref[rows] = total.astype(out_ref.dtype)
            continue
        stage_ref, sems = refs
        stage_ref[rows] = total.astype(stage_ref.dtype)
        stores.append(pltpu.make_async_copy(stage_ref.at[rows], out_ref.at[rows], sems.at[block]))
        stores[-1].start()
    for store in stores:
        store.wait()


def pull(mine, theirs, at=None, so_far=None, dtype=jnp.float32, to_hbm=False):
    rows, width = mine.shape
    args = [mine, *theirs]
    specs = [IN_VMEM] * len(args)
    if at is not None:
        args.insert(0, at)
        specs.insert(0, IN_SMEM)
    if so_far is not None:
        args.append(so_far)
        specs.append(IN_VMEM)
    pairs = rows * sum(part.shape[0] for part in theirs)
    return pl.pallas_call(
        functools.partial(pull_kernel, len(theirs), at is not None, so_far is not None),
        out_shape=jax.ShapeDtypeStruct((rows, width), dtype),
        in_specs=specs,
        out_specs=IN_HBM if to_hbm else IN_VMEM,
        scratch_shapes=[pltpu.VMEM((rows, width), dtype), pltpu.SemaphoreType.DMA((2,))]
        if to_hbm
        else [],
        compiler_params=PARAMS,
        cost_estimate=pl.CostEstimate(
            flops=4 * pairs * width, bytes_accessed=8 * rows * width, transcendentals=2 * pairs
        ),
    )(*args)


def add_kernel(one_ref, two_ref, out_ref, stage_ref, sem):
    stage_ref[...] = (one_ref[...] + two_ref[...].astype(jnp.float32)).astype(jnp.bfloat16)
    copy = pltpu.make_async_copy(stage_ref, out_ref, sem)
    copy.start()
    copy.wait()


def add_rows(one, two):
    return pl.pallas_call(
        add_kernel,
        out_shape=jax.ShapeDtypeStruct(one.shape, jnp.bfloat16),
        in_specs=[IN_VMEM, IN_VMEM],
        out_specs=IN_HBM,
        scratch_shapes=[pltpu.VMEM(one.shape, jnp.bfloat16), pltpu.SemaphoreType.DMA(())],
        compiler_params=PARAMS,
    )(one, two)


def line_sum(back_ref, start, rows, step):
    total = back_ref[start : start + rows].astype(jnp.float32)
    for place in range(1, LINE):
        at = place * step + start
        total = total + back_ref[at : at + rows].astype(jnp.float32)
    return total


def sum_kernel(back_ref, near_ref, far_ref):
    rows = near_ref.shape[0]
    near_ref[...] = line_sum(back_ref, 0, rows, 2 * rows)
    far_ref[...] = line_sum(back_ref, rows, rows, 2 * rows).astype(far_ref.dtype)


def sum_rows(back):
    shape = (back.shape[0] // (2 * LINE), back.shape[1])
    return pl.pallas_call(
        sum_kernel,
        out_shape=(
            jax.ShapeDtypeStruct(shape, jnp.float32),
            jax.ShapeDtypeStruct(shape, jnp.bfloat16),
        ),
        in_specs=[IN_VMEM],
        out_specs=(IN_VMEM, IN_VMEM),
        compiler_params=PARAMS,
    )(back)


def close_kernel(core_ref, back_ref, near_ref, far_ref, images_ref, texts_ref, img_ref, txt_ref):
    first = core_ref[0] == 0
    rows = near_ref.shape[0]
    kept = line_sum(back_ref, 0, rows, rows)
    got = near_ref[...] + far_ref[...].astype(jnp.float32)
    img_ref[...] = raw_grad(jnp.where(first, kept, got), images_ref[...])
    txt_ref[...] = raw_grad(jnp.where(first, got, kept), texts_ref[...])


def close_rows(core, back, near, far, images, texts):
    shape = jax.ShapeDtypeStruct(near.shape, jnp.float32)
    return pl.pallas_call(
        close_kernel,
        out_shape=(shape, shape),
        in_specs=[IN_SMEM] + [IN_VMEM] * 5,
        out_specs=(IN_VMEM, IN_VMEM),
        compiler_params=PARAMS,
    )(core, back, near, far, images, texts)


def in_hbm(array):
    return pltpu.with_memory_space_constraint(array, pltpu.HBM)


def in_vmem(array):
    return pltpu.with_memory_space_constraint(array, pltpu.VMEM)


def local(images, texts):
    rows = images.shape[0]
    bf = jnp.bfloat16
    core = lax.axis_index("core")
    first = core == 0
    y, z = lax.axis_index("y"), lax.axis_index("z")
    my_place, their_place = jnp.where(first, z, y), jnp.where(first, y, z)
    groups = line_groups()
    same_core = across_x(lambda at: at, lambda at: at)
    to_gather = across_x(lambda at: 1 - at, lambda at: 1 - at)
    to_owner = across_x(lambda at: at, lambda at: 1 - at)
    core = core.astype(jnp.int32).reshape(1)

    def trade(blocks):
        return lax.all_to_all(
            blocks, AXES, split_axis=0, concat_axis=0, axis_index_groups=groups, tiled=True
        )

    def send_x(block, pairs):
        return lax.ppermute(block, AXES, pairs)

    def swap_core(block):
        return lax.ppermute(block, "core", SWAP)

    copies_a, other = open_rows(core, in_hbm(images), in_hbm(texts))
    near_a = trade(copies_a)
    from_x = send_x(other, to_gather)
    mine_b = trade(copies(swap_core(other), from_x))
    far_a = send_x(near_a, same_core)
    theirs_a = swap_core(jnp.concatenate([near_a, far_a], 0))

    at_ab = jnp.stack([my_place * rows, their_place * 2 * rows, rows]).astype(jnp.int32)
    at_ba = jnp.stack([my_place * 2 * rows, their_place * rows, rows]).astype(jnp.int32)
    theirs_b = in_vmem(swap_core(mine_b))
    sum_b = pull(mine_b, [theirs_a], at=at_ba, dtype=bf)
    back_b = trade(pull(mine_b, [theirs_b], so_far=sum_b, dtype=bf, to_hbm=True))

    back_x = send_x(pull(in_hbm(far_a), [theirs_a, theirs_b], dtype=bf, to_hbm=True), same_core)
    sum_a = pull(in_hbm(near_a), [theirs_a, theirs_b], at=at_ab)
    back_a = trade(add_rows(sum_a, back_x))

    near, far = sum_rows(back_b)
    far = send_x(far, to_owner)
    return close_rows(core, back_a, swap_core(near), far, images, texts)


def solution(mesh):
    fine = Mesh(mesh.devices.reshape(SIZES), AXES)
    return jax.shard_map(
        local, mesh=fine, in_specs=(ALL, ALL), out_specs=(ALL, ALL), check_vma=False
    )
```

```python
import functools

import jax
import jax.numpy as jnp
from jax import lax
from jax.experimental import pallas as pl
from jax.experimental.pallas import tpu as pltpu
from jax.sharding import Mesh, PartitionSpec as P

logit_scale = 30.0
logit_bias = -5.0
epsilon = 1e-06

AXES = ("xh", "y", "core", "xl", "z")
SIZES = (2, 8, 2, 2, 8)
ALL = P(AXES, None)
SWAP = [(0, 1), (1, 0)]
LINE = 8

IN_VMEM = pl.BlockSpec(memory_space=pltpu.VMEM)
IN_HBM = pl.BlockSpec(memory_space=pltpu.HBM)
IN_ANY = pl.BlockSpec(memory_space=pl.ANY)
IN_SMEM = pl.BlockSpec(memory_space=pltpu.SMEM)
PARAMS = pltpu.CompilerParams(vmem_limit_bytes=16 * 2**20)


def index_of(xh, y, core, xl, z):
    return (((xh * 8 + y) * 2 + core) * 2 + xl) * 8 + z


def line_groups(role):
    groups = []
    for core in range(2):
        for xh in range(2):
            for xl in range(2):
                for at in range(8):
                    if role(core) == 0:
                        groups.append([index_of(xh, at, core, xl, z) for z in range(8)])
                    else:
                        groups.append([index_of(xh, y, core, xl, at) for y in range(8)])
    return groups


def across_x(role):
    pairs = []
    for xh in range(2):
        for y in range(8):
            for core in range(2):
                for xl in range(2):
                    for z in range(8):
                        to = (xh ^ role(core), y, core, 1 - xl, z)
                        pairs.append((index_of(xh, y, core, xl, z), index_of(*to)))
    return pairs


def unit_rows(raw):
    wide = raw.astype(jnp.float32)
    inverse = lax.rsqrt(jnp.sum(wide * wide, axis=1, keepdims=True) + epsilon)
    return (wide * inverse, inverse)


def raw_grad(unit_sum, raw):
    unit, inverse = unit_rows(raw)
    along = jnp.sum(unit_sum * unit, axis=1, keepdims=True)
    return inverse * (unit_sum - along * unit)


def run_all(copies):
    for copy in copies:
        copy.start()
    for copy in copies:
        copy.wait()


def open_kernel(
    core_ref, images_hbm, texts_hbm, copies_ref, second_ref, images_ref, texts_ref, unit_ref, sems
):
    first = core_ref[0] == 0
    run_all(
        [
            pltpu.make_async_copy(images_hbm, images_ref, sems.at[0]),
            pltpu.make_async_copy(texts_hbm, texts_ref, sems.at[1]),
        ]
    )
    img = unit_rows(images_ref[...])[0].astype(jnp.bfloat16)
    txt = unit_rows(texts_ref[...])[0].astype(jnp.bfloat16)
    unit_ref[...] = jnp.where(first, img, txt)
    second_ref[...] = jnp.where(first, txt, img)
    run_all(
        [pltpu.make_async_copy(unit_ref, copies_ref.at[at], sems.at[at]) for at in range(LINE)]
    )


def open_rows(core, images, texts):
    shape = images.shape
    return pl.pallas_call(
        open_kernel,
        out_shape=(
            pltpu.HBM((LINE, *shape), jnp.bfloat16),
            jax.ShapeDtypeStruct(shape, jnp.bfloat16),
        ),
        in_specs=[IN_SMEM, IN_HBM, IN_HBM],
        out_specs=(IN_HBM, IN_VMEM),
        scratch_shapes=[pltpu.VMEM(shape, jnp.bfloat16)] * 3 + [pltpu.SemaphoreType.DMA((LINE,))],
        compiler_params=PARAMS,
    )(core, images, texts)


def copies_kernel(near_ref, far_ref, out_ref, sems):
    rows = near_ref.shape[0]
    copies = []
    for at in range(LINE):
        for half, ref in enumerate((near_ref, far_ref)):
            target = out_ref.at[at, pl.ds(half * rows, rows)]
            copies.append(pltpu.make_async_copy(ref, target, sems.at[2 * at + half]))
    run_all(copies)


def copies(near, far):
    rows, width = near.shape
    return pl.pallas_call(
        copies_kernel,
        out_shape=pltpu.HBM((LINE, 2 * rows, width), near.dtype),
        in_specs=[IN_VMEM, IN_VMEM],
        out_specs=IN_HBM,
        scratch_shapes=[pltpu.SemaphoreType.DMA((2 * LINE,))],
        compiler_params=PARAMS,
    )(near, far)


def hold_kernel(*refs):
    del refs


def hold(kept, after):
    return pl.pallas_call(
        hold_kernel,
        out_shape=jax.ShapeDtypeStruct(kept.shape, kept.dtype),
        in_specs=[IN_ANY] * (1 + len(after)),
        out_specs=IN_ANY,
        input_output_aliases={0: 0},
        compiler_params=PARAMS,
    )(kept, *after)


def block_of(ref, half):
    if half is not None:
        rows = ref.shape[1] // 2
        value = ref[:, half * rows : (half + 1) * rows, :]
    else:
        value = ref[...]
    return value.reshape(-1, value.shape[-1])


def pull_kernel(halves, parts, loads, labelled, added, waits, kind, *refs):
    refs = list(refs)
    at_ref = refs.pop(0) if labelled else None
    mine = [(refs.pop(0), half) for half in halves]
    theirs = [refs.pop(0) for _ in range(parts)]
    so_far_ref = refs.pop(0) if added else None
    if waits:
        refs.pop(0)
    out_ref = refs.pop(0)
    load = None
    if loads:
        loaded_ref, load_sem = refs.pop(0), refs.pop(0)
        load = pltpu.make_async_copy(theirs[-1], loaded_ref, load_sem)
        load.start()
        theirs[-1] = loaded_ref
    stores = []
    for block, (ref, half) in enumerate(mine):
        rows = block_of(ref, half)
        total = None
        for part, theirs_ref in enumerate(theirs):
            if load is not None and part == parts - 1:
                load.wait()
                load = None
            scores = lax.dot_general(
                rows,
                block_of(theirs_ref, None),
                (((1,), (1,)), ((), ())),
                preferred_element_type=jnp.float32,
            )
            chance = 1.0 / (1.0 + jnp.exp(-logit_bias - logit_scale * scores))
            if labelled == (block, part):
                row = lax.broadcasted_iota(jnp.int32, scores.shape, 0) - at_ref[0]
                column = lax.broadcasted_iota(jnp.int32, scores.shape, 1) - at_ref[1]
                same = (row == column) & (row >= 0) & (row < at_ref[2])
                chance = jnp.where(same, chance - 1.0, chance)
            coef = (logit_scale * chance).astype(jnp.bfloat16)
            if kind == "line" and part == parts - 1:
                break
            terms = jnp.dot(coef, block_of(theirs_ref, None), preferred_element_type=jnp.float32)
            total = terms if total is None else total + terms
        size = rows.shape[0]
        if kind == "vmem":
            if added:
                total = total + so_far_ref[block * size : (block + 1) * size].astype(jnp.float32)
            out_ref[block * size : (block + 1) * size] = total.astype(out_ref.dtype)
            continue
        stage_ref, sems = refs
        for half in range(2):
            rows = slice(half * size // 2, (half + 1) * size // 2)
            terms = jnp.dot(
                coef[rows], block_of(theirs[-1], None), preferred_element_type=jnp.float32
            )
            if total is not None:
                terms = terms + total[rows]
            if added:
                terms = terms + so_far_ref[rows].astype(jnp.float32)
            stage_ref[rows] = terms.astype(stage_ref.dtype)
            stores.append(
                pltpu.make_async_copy(stage_ref.at[rows], out_ref.at[rows], sems.at[half])
            )
            stores[-1].start()
    for store in stores:
        store.wait()


def pull(
    mine,
    theirs,
    at=None,
    labelled=None,
    so_far=None,
    after=None,
    load=False,
    kind="vmem",
    dtype=jnp.float32,
):
    halves = [half for _, half in mine]
    width = theirs[0].shape[-1]
    size = sum(part.size for part in theirs) // width
    rows = [part.size // width // (1 if half is None else 2) for part, half in mine]
    args = [part for part, _ in mine] + list(theirs)
    specs = [IN_VMEM] * len(args)
    if load:
        specs[-1] = IN_HBM
    if labelled:
        args.insert(0, at)
        specs.insert(0, IN_SMEM)
    if so_far is not None:
        args.append(so_far)
        specs.append(IN_VMEM)
    if after is not None:
        args.append(after)
        specs.append(IN_ANY)
    shape, scratch = (sum(rows), width), []
    if load:
        scratch += [pltpu.VMEM(theirs[-1].shape, jnp.bfloat16), pltpu.SemaphoreType.DMA(())]
    if kind == "line":
        scratch += [pltpu.VMEM(shape, dtype), pltpu.SemaphoreType.DMA((2,))]
    return pl.pallas_call(
        functools.partial(
            pull_kernel,
            halves,
            len(theirs),
            load,
            labelled,
            so_far is not None,
            after is not None,
            kind,
        ),
        out_shape=(jax.ShapeDtypeStruct if kind == "vmem" else pltpu.HBM)(shape, dtype),
        in_specs=specs,
        out_specs=IN_VMEM if kind == "vmem" else IN_HBM,
        scratch_shapes=scratch,
        compiler_params=PARAMS,
        cost_estimate=pl.CostEstimate(
            flops=4 * sum(rows) * size * width,
            bytes_accessed=8 * sum(rows) * width,
            transcendentals=2 * sum(rows) * size,
        ),
    )(*args)


def add_kernel(one_ref, two_ref, out_ref, stage_ref, sem):
    total = (one_ref[...] + two_ref[...].astype(jnp.float32)).astype(jnp.bfloat16)
    stage_ref[...] = total.reshape(stage_ref.shape)
    run_all([pltpu.make_async_copy(stage_ref, out_ref, sem)])


def add_rows(one, two):
    shape = (LINE, one.shape[0] // LINE, one.shape[1])
    return pl.pallas_call(
        add_kernel,
        out_shape=pltpu.HBM(shape, jnp.bfloat16),
        in_specs=[IN_VMEM, IN_VMEM],
        out_specs=IN_HBM,
        scratch_shapes=[pltpu.VMEM(shape, jnp.bfloat16), pltpu.SemaphoreType.DMA(())],
        compiler_params=PARAMS,
    )(one, two)


def line_sum(back_ref, start, rows):
    total = back_ref[0, start : start + rows].astype(jnp.float32)
    for place in range(1, LINE):
        total = total + back_ref[place, start : start + rows].astype(jnp.float32)
    return total


def sum_kernel(back_ref, near_ref, far_ref):
    rows = near_ref.shape[0]
    near_ref[...] = line_sum(back_ref, 0, rows)
    far_ref[...] = line_sum(back_ref, rows, rows).astype(far_ref.dtype)


def sum_rows(back):
    shape = (back.shape[1] // 2, back.shape[2])
    return pl.pallas_call(
        sum_kernel,
        out_shape=(
            jax.ShapeDtypeStruct(shape, jnp.float32),
            jax.ShapeDtypeStruct(shape, jnp.bfloat16),
        ),
        in_specs=[IN_VMEM],
        out_specs=(IN_VMEM, IN_VMEM),
        compiler_params=PARAMS,
    )(back)


def close_kernel(core_ref, near_ref, far_ref, back_ref, images_ref, texts_ref, img_ref, txt_ref):
    first = core_ref[0] == 0
    q_sum = near_ref[...] + far_ref[...].astype(jnp.float32)
    p_sum = line_sum(back_ref, 0, near_ref.shape[0])
    img_ref[...] = raw_grad(jnp.where(first, p_sum, q_sum), images_ref[...])
    txt_ref[...] = raw_grad(jnp.where(first, q_sum, p_sum), texts_ref[...])


def close_rows(core, near, far, back, images, texts):
    shape = jax.ShapeDtypeStruct(near.shape, jnp.float32)
    return pl.pallas_call(
        close_kernel,
        out_shape=(shape, shape),
        in_specs=[IN_SMEM] + [IN_VMEM] * 5,
        out_specs=(IN_VMEM, IN_VMEM),
        compiler_params=PARAMS,
    )(core, near, far, back, images, texts)


def in_hbm(array):
    return pltpu.with_memory_space_constraint(array, pltpu.HBM)


def in_vmem(array):
    return pltpu.with_memory_space_constraint(array, pltpu.VMEM)


def trade(blocks, role):
    return lax.all_to_all(
        blocks, AXES, split_axis=0, concat_axis=0, axis_index_groups=line_groups(role), tiled=True
    )


def swap_x(block, role):
    return lax.ppermute(block, AXES, across_x(role))


def p_role(core):
    return core


def q_role(core):
    return 1 - core


def local(images, texts):
    rows, width = images.shape
    bf = jnp.bfloat16
    core = lax.axis_index("core")
    y, z = lax.axis_index("y"), lax.axis_index("z")
    p_place, q_place = jnp.where(core == 0, z, y), jnp.where(core == 0, y, z)
    core = core.astype(jnp.int32).reshape(1)

    copies_p, own_q = open_rows(core, in_hbm(images), in_hbm(texts))
    near_p = trade(copies_p, p_role).reshape(-1, width)
    copies_q = copies(own_q, swap_x(own_q, q_role))
    near_p = hold(near_p, [in_hbm(copies_q)])
    mine_q = trade(copies_q, q_role)
    far_p = swap_x(near_p, p_role)
    theirs_p = in_hbm(lax.ppermute(jnp.concatenate([near_p, far_p], 0), "core", SWAP))

    at_pq = jnp.stack([p_place * rows, q_place * 2 * rows, rows]).astype(jnp.int32)
    at_qp = jnp.stack([q_place * 2 * rows, p_place * rows, rows]).astype(jnp.int32)
    all_q = [(mine_q, None)]
    theirs_q = in_vmem(lax.ppermute(mine_q.reshape(-1, width), "core", SWAP))
    sum_q = pull(all_q, [near_p, far_p], at=at_qp, labelled=(0, 0), after=theirs_p, dtype=bf)
    sum_q = pull(all_q, [theirs_q], so_far=sum_q, kind="line", dtype=bf)
    near, far = sum_rows(trade(sum_q.reshape(mine_q.shape), q_role))
    far = swap_x(far, q_role)

    others = [mine_q, theirs_p]
    back_p = swap_x(pull([(far_p, None)], others, load=True, dtype=bf), p_role)
    near_p = pull([(near_p, None)], others, at=at_pq, labelled=(0, 0), load=True)
    back_p = trade(add_rows(near_p, back_p), p_role)
    return close_rows(core, near, far, back_p, images, texts)


def solution(mesh):
    fine = Mesh(mesh.devices.reshape(SIZES), AXES)
    return jax.shard_map(
        local, mesh=fine, in_specs=(ALL, ALL), out_specs=(ALL, ALL), check_vma=False
    )
```

```python
import functools

import jax
import jax.numpy as jnp
from jax import lax
from jax.experimental import pallas as pl
from jax.experimental.pallas import tpu as pltpu
from jax.sharding import Mesh, PartitionSpec as P

logit_scale = 30.0
logit_bias = -5.0
epsilon = 1e-06

AXES = ("xh", "y", "core", "xl", "z")
SIZES = (2, 8, 2, 2, 8)
ALL = P(AXES, None)
SWAP = [(0, 1), (1, 0)]
LINE = 8
P_ORDER = (0, 1, 4, 5, 2, 3, 6, 7)
Q_ORDER = (0, 4, 2, 6, 5, 1, 7, 3)

IN_VMEM = pl.BlockSpec(memory_space=pltpu.VMEM)
IN_HBM = pl.BlockSpec(memory_space=pltpu.HBM)
IN_ANY = pl.BlockSpec(memory_space=pl.ANY)
IN_SMEM = pl.BlockSpec(memory_space=pltpu.SMEM)
PARAMS = pltpu.CompilerParams(vmem_limit_bytes=16 * 2**20)


def index_of(xh, y, core, xl, z):
    return (((xh * 8 + y) * 2 + core) * 2 + xl) * 8 + z


def line_groups(role, order):
    groups = []
    for core in range(2):
        for xh in range(2):
            for xl in range(2):
                for at in range(8):
                    if role(core) == 0:
                        groups.append([index_of(xh, at, core, xl, z) for z in order])
                    else:
                        groups.append([index_of(xh, y, core, xl, at) for y in order])
    return groups


def across_x(role):
    pairs = []
    for xh in range(2):
        for y in range(8):
            for core in range(2):
                for xl in range(2):
                    for z in range(8):
                        to = (xh ^ role(core), y, core, 1 - xl, z)
                        pairs.append((index_of(xh, y, core, xl, z), index_of(*to)))
    return pairs


def unit_rows(raw):
    wide = raw.astype(jnp.float32)
    inverse = lax.rsqrt(jnp.sum(wide * wide, axis=1, keepdims=True) + epsilon)
    return (wide * inverse, inverse)


def raw_grad(unit_sum, raw):
    unit, inverse = unit_rows(raw)
    along = jnp.sum(unit_sum * unit, axis=1, keepdims=True)
    return inverse * (unit_sum - along * unit)


def run_all(copies):
    for copy in copies:
        copy.start()
    for copy in copies:
        copy.wait()


def open_kernel(
    core_ref, images_hbm, texts_hbm, copies_ref, second_ref, images_ref, texts_ref, unit_ref, sems
):
    first = core_ref[0] == 0
    run_all(
        [
            pltpu.make_async_copy(images_hbm, images_ref, sems.at[0]),
            pltpu.make_async_copy(texts_hbm, texts_ref, sems.at[1]),
        ]
    )
    img = unit_rows(images_ref[...])[0].astype(jnp.bfloat16)
    txt = unit_rows(texts_ref[...])[0].astype(jnp.bfloat16)
    unit_ref[...] = jnp.where(first, img, txt)
    second_ref[...] = jnp.where(first, txt, img)
    run_all(
        [pltpu.make_async_copy(unit_ref, copies_ref.at[at], sems.at[at]) for at in range(LINE)]
    )


def open_rows(core, images, texts):
    shape = images.shape
    return pl.pallas_call(
        open_kernel,
        out_shape=(
            pltpu.HBM((LINE, *shape), jnp.bfloat16),
            jax.ShapeDtypeStruct(shape, jnp.bfloat16),
        ),
        in_specs=[IN_SMEM, IN_HBM, IN_HBM],
        out_specs=(IN_HBM, IN_VMEM),
        scratch_shapes=[pltpu.VMEM(shape, jnp.bfloat16)] * 3 + [pltpu.SemaphoreType.DMA((LINE,))],
        compiler_params=PARAMS,
    )(core, images, texts)


def copies_kernel(near_ref, far_ref, out_ref, sems):
    rows = near_ref.shape[0]
    copies = []
    for at in range(LINE):
        for half, ref in enumerate((near_ref, far_ref)):
            target = out_ref.at[at, pl.ds(half * rows, rows)]
            copies.append(pltpu.make_async_copy(ref, target, sems.at[2 * at + half]))
    run_all(copies)


def copies(near, far):
    rows, width = near.shape
    return pl.pallas_call(
        copies_kernel,
        out_shape=pltpu.HBM((LINE, 2 * rows, width), near.dtype),
        in_specs=[IN_VMEM, IN_VMEM],
        out_specs=IN_HBM,
        scratch_shapes=[pltpu.SemaphoreType.DMA((2 * LINE,))],
        compiler_params=PARAMS,
    )(near, far)


def hold_kernel(*refs):
    del refs


def hold(kept, after):
    return pl.pallas_call(
        hold_kernel,
        out_shape=jax.ShapeDtypeStruct(kept.shape, kept.dtype),
        in_specs=[IN_ANY] * (1 + len(after)),
        out_specs=IN_ANY,
        input_output_aliases={0: 0},
        compiler_params=PARAMS,
    )(kept, *after)


def block_of(ref, half):
    if half is not None:
        rows = ref.shape[1] // 2
        value = ref[:, half * rows : (half + 1) * rows, :]
    else:
        value = ref[...]
    return value.reshape(-1, value.shape[-1])


def pull_kernel(halves, parts, loads, labelled, added, waits, kind, *refs):
    refs = list(refs)
    at_ref = refs.pop(0) if labelled else None
    mine = [(refs.pop(0), half) for half in halves]
    theirs = [refs.pop(0) for _ in range(parts)]
    so_far_ref = refs.pop(0) if added else None
    if waits:
        refs.pop(0)
    out_ref = refs.pop(0)
    load = None
    if loads:
        loaded_ref, load_sem = refs.pop(0), refs.pop(0)
        load = pltpu.make_async_copy(theirs[-1], loaded_ref, load_sem)
        load.start()
        theirs[-1] = loaded_ref
    stores = []
    for block, (ref, half) in enumerate(mine):
        rows = block_of(ref, half)
        total = None
        for part, theirs_ref in enumerate(theirs):
            if load is not None and part == parts - 1:
                load.wait()
                load = None
            scores = lax.dot_general(
                rows,
                block_of(theirs_ref, None),
                (((1,), (1,)), ((), ())),
                preferred_element_type=jnp.float32,
            )
            chance = 1.0 / (1.0 + jnp.exp(-logit_bias - logit_scale * scores))
            if labelled == (block, part):
                row = lax.broadcasted_iota(jnp.int32, scores.shape, 0) - at_ref[0]
                column = lax.broadcasted_iota(jnp.int32, scores.shape, 1) - at_ref[1]
                same = (row == column) & (row >= 0) & (row < at_ref[2])
                chance = jnp.where(same, chance - 1.0, chance)
            coef = (logit_scale * chance).astype(jnp.bfloat16)
            if kind == "line" and part == parts - 1:
                break
            terms = jnp.dot(coef, block_of(theirs_ref, None), preferred_element_type=jnp.float32)
            total = terms if total is None else total + terms
        size = rows.shape[0]
        if kind == "vmem":
            if added:
                total = total + so_far_ref[block * size : (block + 1) * size].astype(jnp.float32)
            out_ref[block * size : (block + 1) * size] = total.astype(out_ref.dtype)
            continue
        stage_ref, sems = refs
        for half in range(2):
            rows = slice(half * size // 2, (half + 1) * size // 2)
            terms = jnp.dot(
                coef[rows], block_of(theirs[-1], None), preferred_element_type=jnp.float32
            )
            if total is not None:
                terms = terms + total[rows]
            if added:
                terms = terms + so_far_ref[rows].astype(jnp.float32)
            stage_ref[rows] = terms.astype(stage_ref.dtype)
            stores.append(
                pltpu.make_async_copy(stage_ref.at[rows], out_ref.at[rows], sems.at[half])
            )
            stores[-1].start()
    for store in stores:
        store.wait()


def pull(
    mine,
    theirs,
    at=None,
    labelled=None,
    so_far=None,
    after=None,
    load=False,
    kind="vmem",
    dtype=jnp.float32,
):
    halves = [half for _, half in mine]
    width = theirs[0].shape[-1]
    size = sum(part.size for part in theirs) // width
    rows = [part.size // width // (1 if half is None else 2) for part, half in mine]
    args = [part for part, _ in mine] + list(theirs)
    specs = [IN_VMEM] * len(args)
    if load:
        specs[-1] = IN_HBM
    if labelled:
        args.insert(0, at)
        specs.insert(0, IN_SMEM)
    if so_far is not None:
        args.append(so_far)
        specs.append(IN_VMEM)
    if after is not None:
        args.append(after)
        specs.append(IN_ANY)
    shape, scratch = (sum(rows), width), []
    if load:
        scratch += [pltpu.VMEM(theirs[-1].shape, jnp.bfloat16), pltpu.SemaphoreType.DMA(())]
    if kind == "line":
        scratch += [pltpu.VMEM(shape, dtype), pltpu.SemaphoreType.DMA((2,))]
    return pl.pallas_call(
        functools.partial(
            pull_kernel,
            halves,
            len(theirs),
            load,
            labelled,
            so_far is not None,
            after is not None,
            kind,
        ),
        out_shape=(jax.ShapeDtypeStruct if kind == "vmem" else pltpu.HBM)(shape, dtype),
        in_specs=specs,
        out_specs=IN_VMEM if kind == "vmem" else IN_HBM,
        scratch_shapes=scratch,
        compiler_params=PARAMS,
        cost_estimate=pl.CostEstimate(
            flops=4 * sum(rows) * size * width,
            bytes_accessed=8 * sum(rows) * width,
            transcendentals=2 * sum(rows) * size,
        ),
    )(*args)


def add_kernel(one_ref, two_ref, out_ref, stage_ref, sem):
    total = (one_ref[...] + two_ref[...].astype(jnp.float32)).astype(jnp.bfloat16)
    stage_ref[...] = total.reshape(stage_ref.shape)
    run_all([pltpu.make_async_copy(stage_ref, out_ref, sem)])


def add_rows(one, two):
    shape = (LINE, one.shape[0] // LINE, one.shape[1])
    return pl.pallas_call(
        add_kernel,
        out_shape=pltpu.HBM(shape, jnp.bfloat16),
        in_specs=[IN_VMEM, IN_VMEM],
        out_specs=IN_HBM,
        scratch_shapes=[pltpu.VMEM(shape, jnp.bfloat16), pltpu.SemaphoreType.DMA(())],
        compiler_params=PARAMS,
    )(one, two)


def line_sum(back_ref, start, rows):
    total = back_ref[0, start : start + rows].astype(jnp.float32)
    for place in range(1, LINE):
        total = total + back_ref[place, start : start + rows].astype(jnp.float32)
    return total


def sum_kernel(back_ref, near_ref, far_ref):
    rows = near_ref.shape[0]
    near_ref[...] = line_sum(back_ref, 0, rows)
    far_ref[...] = line_sum(back_ref, rows, rows).astype(far_ref.dtype)


def sum_rows(back):
    shape = (back.shape[1] // 2, back.shape[2])
    return pl.pallas_call(
        sum_kernel,
        out_shape=(
            jax.ShapeDtypeStruct(shape, jnp.float32),
            jax.ShapeDtypeStruct(shape, jnp.bfloat16),
        ),
        in_specs=[IN_VMEM],
        out_specs=(IN_VMEM, IN_VMEM),
        compiler_params=PARAMS,
    )(back)


def close_kernel(core_ref, near_ref, far_ref, back_ref, images_ref, texts_ref, img_ref, txt_ref):
    first = core_ref[0] == 0
    q_sum = near_ref[...] + far_ref[...].astype(jnp.float32)
    p_sum = line_sum(back_ref, 0, near_ref.shape[0])
    img_ref[...] = raw_grad(jnp.where(first, p_sum, q_sum), images_ref[...])
    txt_ref[...] = raw_grad(jnp.where(first, q_sum, p_sum), texts_ref[...])


def close_rows(core, near, far, back, images, texts):
    shape = jax.ShapeDtypeStruct(near.shape, jnp.float32)
    return pl.pallas_call(
        close_kernel,
        out_shape=(shape, shape),
        in_specs=[IN_SMEM] + [IN_VMEM] * 5,
        out_specs=(IN_VMEM, IN_VMEM),
        compiler_params=PARAMS,
    )(core, near, far, back, images, texts)


def in_hbm(array):
    return pltpu.with_memory_space_constraint(array, pltpu.HBM)


def in_vmem(array):
    return pltpu.with_memory_space_constraint(array, pltpu.VMEM)


def trade(blocks, role, order):
    groups = line_groups(role, order)
    return lax.all_to_all(
        blocks, AXES, split_axis=0, concat_axis=0, axis_index_groups=groups, tiled=True
    )


def place_in(order, at):
    return sum(jnp.where(at == where, place, 0) for place, where in enumerate(order))


def swap_x(block, role):
    return lax.ppermute(block, AXES, across_x(role))


def p_role(core):
    return core


def q_role(core):
    return 1 - core


def local(images, texts):
    rows, width = images.shape
    bf = jnp.bfloat16
    core = lax.axis_index("core")
    y, z = lax.axis_index("y"), lax.axis_index("z")
    p_place = place_in(P_ORDER, jnp.where(core == 0, z, y))
    q_place = place_in(Q_ORDER, jnp.where(core == 0, y, z))
    core = core.astype(jnp.int32).reshape(1)

    copies_p, own_q = open_rows(core, in_hbm(images), in_hbm(texts))
    near_p = trade(copies_p, p_role, P_ORDER).reshape(-1, width)
    copies_q = copies(own_q, swap_x(own_q, q_role))
    near_p = hold(near_p, [in_hbm(copies_q)])
    mine_q = trade(copies_q, q_role, Q_ORDER)
    far_p = swap_x(near_p, p_role)
    theirs_p = in_hbm(lax.ppermute(jnp.concatenate([near_p, far_p], 0), "core", SWAP))

    at_pq = jnp.stack([p_place * rows, q_place * 2 * rows, rows]).astype(jnp.int32)
    at_qp = jnp.stack([q_place * 2 * rows, p_place * rows, rows]).astype(jnp.int32)
    all_q = [(mine_q, None)]
    theirs_q = in_vmem(lax.ppermute(mine_q.reshape(-1, width), "core", SWAP))
    sum_q = pull(all_q, [near_p, far_p], at=at_qp, labelled=(0, 0), after=theirs_p, dtype=bf)
    sum_q = pull(all_q, [theirs_q], so_far=sum_q, kind="line", dtype=bf)
    near, far = sum_rows(trade(sum_q.reshape(mine_q.shape), q_role, Q_ORDER))
    far = swap_x(far, q_role)

    others = [mine_q, theirs_p]
    back_p = swap_x(pull([(far_p, None)], others, load=True, dtype=bf), p_role)
    near_p = pull([(near_p, None)], others, at=at_pq, labelled=(0, 0), load=True)
    back_p = trade(add_rows(near_p, back_p), p_role, P_ORDER)
    return close_rows(core, near, far, back_p, images, texts)


def solution(mesh):
    fine = Mesh(mesh.devices.reshape(SIZES), AXES)
    return jax.shard_map(
        local, mesh=fine, in_specs=(ALL, ALL), out_specs=(ALL, ALL), check_vma=False
    )
```

```python
import functools

import jax
import jax.numpy as jnp
from jax import lax
from jax.experimental import pallas as pl
from jax.experimental.pallas import tpu as pltpu
from jax.sharding import Mesh, PartitionSpec as P

logit_scale = 30.0
logit_bias = -5.0
epsilon = 1e-06

AXES = ("xh", "y", "core", "xl", "z")
SIZES = (2, 8, 2, 2, 8)
ALL = P(AXES, None)
SWAP = [(0, 1), (1, 0)]
LINE = 8
P_ORDER = (0, 4, 2, 6, 3, 7, 1, 5)
Q_ORDER = (0, 2, 4, 6, 1, 3, 5, 7)

IN_VMEM = pl.BlockSpec(memory_space=pltpu.VMEM)
IN_HBM = pl.BlockSpec(memory_space=pltpu.HBM)
IN_ANY = pl.BlockSpec(memory_space=pl.ANY)
IN_SMEM = pl.BlockSpec(memory_space=pltpu.SMEM)
PARAMS = pltpu.CompilerParams(vmem_limit_bytes=16 * 2**20)


def index_of(xh, y, core, xl, z):
    return (((xh * 8 + y) * 2 + core) * 2 + xl) * 8 + z


def line_groups(role, order):
    groups = []
    for core in range(2):
        for xh in range(2):
            for xl in range(2):
                for at in range(8):
                    if role(core) == 0:
                        groups.append([index_of(xh, at, core, xl, z) for z in order])
                    else:
                        groups.append([index_of(xh, y, core, xl, at) for y in order])
    return groups


def across_x(role):
    pairs = []
    for xh in range(2):
        for y in range(8):
            for core in range(2):
                for xl in range(2):
                    for z in range(8):
                        to = (xh ^ role(core), y, core, 1 - xl, z)
                        pairs.append((index_of(xh, y, core, xl, z), index_of(*to)))
    return pairs


def unit_rows(raw):
    wide = raw.astype(jnp.float32)
    inverse = lax.rsqrt(jnp.sum(wide * wide, axis=1, keepdims=True) + epsilon)
    return (wide * inverse, inverse)


def raw_grad(unit_sum, raw):
    unit, inverse = unit_rows(raw)
    along = jnp.sum(unit_sum * unit, axis=1, keepdims=True)
    return inverse * (unit_sum - along * unit)


def run_all(copies):
    for copy in copies:
        copy.start()
    for copy in copies:
        copy.wait()


def open_kernel(
    core_ref, images_hbm, texts_hbm, copies_ref, second_ref, images_ref, texts_ref, unit_ref, sems
):
    first = core_ref[0] == 0
    run_all(
        [
            pltpu.make_async_copy(images_hbm, images_ref, sems.at[0]),
            pltpu.make_async_copy(texts_hbm, texts_ref, sems.at[1]),
        ]
    )
    p_raw = jnp.where(first, images_ref[...], texts_ref[...])
    q_raw = jnp.where(first, texts_ref[...], images_ref[...])
    unit_ref[...] = unit_rows(p_raw)[0].astype(jnp.bfloat16)
    stores = [
        pltpu.make_async_copy(unit_ref, copies_ref.at[at], sems.at[at]) for at in range(LINE)
    ]
    for store in stores:
        store.start()
    second_ref[...] = unit_rows(q_raw)[0].astype(jnp.bfloat16)
    for store in stores:
        store.wait()


def open_rows(core, images, texts):
    shape = images.shape
    return pl.pallas_call(
        open_kernel,
        out_shape=(
            pltpu.HBM((LINE, *shape), jnp.bfloat16),
            jax.ShapeDtypeStruct(shape, jnp.bfloat16),
        ),
        in_specs=[IN_SMEM, IN_HBM, IN_HBM],
        out_specs=(IN_HBM, IN_VMEM),
        scratch_shapes=[pltpu.VMEM(shape, jnp.bfloat16)] * 3 + [pltpu.SemaphoreType.DMA((LINE,))],
        compiler_params=PARAMS,
    )(core, images, texts)


def copies_kernel(near_ref, far_ref, out_ref, sems):
    rows = near_ref.shape[0]
    copies = []
    for at in range(LINE):
        for half, ref in enumerate((near_ref, far_ref)):
            target = out_ref.at[at, pl.ds(half * rows, rows)]
            copies.append(pltpu.make_async_copy(ref, target, sems.at[2 * at + half]))
    run_all(copies)


def copies(near, far):
    rows, width = near.shape
    return pl.pallas_call(
        copies_kernel,
        out_shape=pltpu.HBM((LINE, 2 * rows, width), near.dtype),
        in_specs=[IN_VMEM, IN_VMEM],
        out_specs=IN_HBM,
        scratch_shapes=[pltpu.SemaphoreType.DMA((2 * LINE,))],
        compiler_params=PARAMS,
    )(near, far)


def hold_kernel(*refs):
    del refs


def hold(kept, after):
    return pl.pallas_call(
        hold_kernel,
        out_shape=jax.ShapeDtypeStruct(kept.shape, kept.dtype),
        in_specs=[IN_ANY] * (1 + len(after)),
        out_specs=IN_ANY,
        input_output_aliases={0: 0},
        compiler_params=PARAMS,
    )(kept, *after)


def block_of(ref, half):
    if half is not None:
        rows = ref.shape[1] // 2
        value = ref[:, half * rows : (half + 1) * rows, :]
    else:
        value = ref[...]
    return value.reshape(-1, value.shape[-1])


def pull_kernel(halves, parts, loads, labelled, added, waits, kind, *refs):
    refs = list(refs)
    at_ref = refs.pop(0) if labelled else None
    mine = [(refs.pop(0), half) for half in halves]
    theirs = [refs.pop(0) for _ in range(parts)]
    so_far_ref = refs.pop(0) if added else None
    if waits:
        refs.pop(0)
    out_ref = refs.pop(0)
    load = None
    if loads:
        loaded_ref, load_sem = refs.pop(0), refs.pop(0)
        load = pltpu.make_async_copy(theirs[-1], loaded_ref, load_sem)
        load.start()
        theirs[-1] = loaded_ref
    stores = []
    for block, (ref, half) in enumerate(mine):
        rows = block_of(ref, half)
        total = None
        for part, theirs_ref in enumerate(theirs):
            if load is not None and part == parts - 1:
                load.wait()
                load = None
            scores = lax.dot_general(
                rows,
                block_of(theirs_ref, None),
                (((1,), (1,)), ((), ())),
                preferred_element_type=jnp.float32,
            )
            chance = 1.0 / (1.0 + jnp.exp(-logit_bias - logit_scale * scores))
            if labelled == (block, part):
                row = lax.broadcasted_iota(jnp.int32, scores.shape, 0) - at_ref[0]
                column = lax.broadcasted_iota(jnp.int32, scores.shape, 1) - at_ref[1]
                same = (row == column) & (row >= 0) & (row < at_ref[2])
                chance = jnp.where(same, chance - 1.0, chance)
            coef = (logit_scale * chance).astype(jnp.bfloat16)
            if kind == "line" and part == parts - 1:
                break
            terms = jnp.dot(coef, block_of(theirs_ref, None), preferred_element_type=jnp.float32)
            total = terms if total is None else total + terms
        size = rows.shape[0]
        if kind == "vmem":
            if added:
                total = total + so_far_ref[block * size : (block + 1) * size].astype(jnp.float32)
            out_ref[block * size : (block + 1) * size] = total.astype(out_ref.dtype)
            continue
        stage_ref, sems = refs
        for half in range(2):
            rows = slice(half * size // 2, (half + 1) * size // 2)
            terms = jnp.dot(
                coef[rows], block_of(theirs[-1], None), preferred_element_type=jnp.float32
            )
            if total is not None:
                terms = terms + total[rows]
            if added:
                terms = terms + so_far_ref[rows].astype(jnp.float32)
            stage_ref[rows] = terms.astype(stage_ref.dtype)
            stores.append(
                pltpu.make_async_copy(stage_ref.at[rows], out_ref.at[rows], sems.at[half])
            )
            stores[-1].start()
    for store in stores:
        store.wait()


def pull(
    mine,
    theirs,
    at=None,
    labelled=None,
    so_far=None,
    after=None,
    load=False,
    kind="vmem",
    dtype=jnp.float32,
):
    halves = [half for _, half in mine]
    width = theirs[0].shape[-1]
    size = sum(part.size for part in theirs) // width
    rows = [part.size // width // (1 if half is None else 2) for part, half in mine]
    args = [part for part, _ in mine] + list(theirs)
    specs = [IN_VMEM] * len(args)
    if load:
        specs[-1] = IN_HBM
    if labelled:
        args.insert(0, at)
        specs.insert(0, IN_SMEM)
    if so_far is not None:
        args.append(so_far)
        specs.append(IN_VMEM)
    if after is not None:
        args.append(after)
        specs.append(IN_ANY)
    shape, scratch = (sum(rows), width), []
    if load:
        scratch += [pltpu.VMEM(theirs[-1].shape, jnp.bfloat16), pltpu.SemaphoreType.DMA(())]
    if kind == "line":
        scratch += [pltpu.VMEM(shape, dtype), pltpu.SemaphoreType.DMA((2,))]
    return pl.pallas_call(
        functools.partial(
            pull_kernel,
            halves,
            len(theirs),
            load,
            labelled,
            so_far is not None,
            after is not None,
            kind,
        ),
        out_shape=(jax.ShapeDtypeStruct if kind == "vmem" else pltpu.HBM)(shape, dtype),
        in_specs=specs,
        out_specs=IN_VMEM if kind == "vmem" else IN_HBM,
        scratch_shapes=scratch,
        compiler_params=PARAMS,
        cost_estimate=pl.CostEstimate(
            flops=4 * sum(rows) * size * width,
            bytes_accessed=8 * sum(rows) * width,
            transcendentals=2 * sum(rows) * size,
        ),
    )(*args)


def add_kernel(one_ref, two_ref, out_ref, stage_ref, sem):
    total = (one_ref[...] + two_ref[...].astype(jnp.float32)).astype(jnp.bfloat16)
    stage_ref[...] = total.reshape(stage_ref.shape)
    run_all([pltpu.make_async_copy(stage_ref, out_ref, sem)])


def add_rows(one, two):
    shape = (LINE, one.shape[0] // LINE, one.shape[1])
    return pl.pallas_call(
        add_kernel,
        out_shape=pltpu.HBM(shape, jnp.bfloat16),
        in_specs=[IN_VMEM, IN_VMEM],
        out_specs=IN_HBM,
        scratch_shapes=[pltpu.VMEM(shape, jnp.bfloat16), pltpu.SemaphoreType.DMA(())],
        compiler_params=PARAMS,
    )(one, two)


def line_sum(back_ref, start, rows):
    total = back_ref[0, start : start + rows].astype(jnp.float32)
    for place in range(1, LINE):
        total = total + back_ref[place, start : start + rows].astype(jnp.float32)
    return total


def sum_kernel(back_ref, near_ref, far_ref):
    rows = near_ref.shape[0]
    near_ref[...] = line_sum(back_ref, 0, rows)
    far_ref[...] = line_sum(back_ref, rows, rows).astype(far_ref.dtype)


def sum_rows(back):
    shape = (back.shape[1] // 2, back.shape[2])
    return pl.pallas_call(
        sum_kernel,
        out_shape=(
            jax.ShapeDtypeStruct(shape, jnp.float32),
            jax.ShapeDtypeStruct(shape, jnp.bfloat16),
        ),
        in_specs=[IN_VMEM],
        out_specs=(IN_VMEM, IN_VMEM),
        compiler_params=PARAMS,
    )(back)


def close_kernel(core_ref, near_ref, far_ref, back_ref, images_ref, texts_ref, img_ref, txt_ref):
    first = core_ref[0] == 0
    q_sum = near_ref[...] + far_ref[...].astype(jnp.float32)
    p_sum = line_sum(back_ref, 0, near_ref.shape[0])
    img_ref[...] = raw_grad(jnp.where(first, p_sum, q_sum), images_ref[...])
    txt_ref[...] = raw_grad(jnp.where(first, q_sum, p_sum), texts_ref[...])


def close_rows(core, near, far, back, images, texts):
    shape = jax.ShapeDtypeStruct(near.shape, jnp.float32)
    return pl.pallas_call(
        close_kernel,
        out_shape=(shape, shape),
        in_specs=[IN_SMEM] + [IN_VMEM] * 5,
        out_specs=(IN_VMEM, IN_VMEM),
        compiler_params=PARAMS,
    )(core, near, far, back, images, texts)


def in_hbm(array):
    return pltpu.with_memory_space_constraint(array, pltpu.HBM)


def in_vmem(array):
    return pltpu.with_memory_space_constraint(array, pltpu.VMEM)


def trade(blocks, role, order):
    groups = line_groups(role, order)
    return lax.all_to_all(
        blocks, AXES, split_axis=0, concat_axis=0, axis_index_groups=groups, tiled=True
    )


def place_in(order, at):
    return sum(jnp.where(at == where, place, 0) for place, where in enumerate(order))


def swap_x(block, role):
    return lax.ppermute(block, AXES, across_x(role))


def p_role(core):
    return core


def q_role(core):
    return 1 - core


def local(images, texts):
    rows, width = images.shape
    bf = jnp.bfloat16
    core = lax.axis_index("core")
    y, z = lax.axis_index("y"), lax.axis_index("z")
    p_place = place_in(P_ORDER, jnp.where(core == 0, z, y))
    q_place = place_in(Q_ORDER, jnp.where(core == 0, y, z))
    core = core.astype(jnp.int32).reshape(1)

    copies_p, own_q = open_rows(core, in_hbm(images), in_hbm(texts))
    near_p = trade(copies_p, p_role, P_ORDER).reshape(-1, width)
    copies_q = copies(own_q, swap_x(own_q, q_role))
    near_p = hold(near_p, [in_hbm(copies_q)])
    mine_q = trade(copies_q, q_role, Q_ORDER)
    far_p = swap_x(near_p, p_role)
    theirs_p = in_hbm(lax.ppermute(jnp.concatenate([near_p, far_p], 0), "core", SWAP))

    at_pq = jnp.stack([p_place * rows, q_place * 2 * rows, rows]).astype(jnp.int32)
    at_qp = jnp.stack([q_place * 2 * rows, p_place * rows, rows]).astype(jnp.int32)
    all_q = [(mine_q, None)]
    theirs_q = in_vmem(lax.ppermute(mine_q.reshape(-1, width), "core", SWAP))
    sum_q = pull(all_q, [near_p, far_p], at=at_qp, labelled=(0, 0), after=theirs_p, dtype=bf)
    sum_q = pull(all_q, [theirs_q], so_far=sum_q, kind="line", dtype=bf)
    near, far = sum_rows(trade(sum_q.reshape(mine_q.shape), q_role, Q_ORDER))
    far = swap_x(far, q_role)

    others = [mine_q, theirs_p]
    back_p = swap_x(pull([(far_p, None)], others, load=True, dtype=bf), p_role)
    near_p = pull([(near_p, None)], others, at=at_pq, labelled=(0, 0), load=True)
    back_p = trade(add_rows(near_p, back_p), p_role, P_ORDER)
    return close_rows(core, near, far, back_p, images, texts)


def solution(mesh):
    fine = Mesh(mesh.devices.reshape(SIZES), AXES)
    return jax.shard_map(
        local, mesh=fine, in_specs=(ALL, ALL), out_specs=(ALL, ALL), check_vma=False
    )
```

```python
import functools

import jax
import jax.numpy as jnp
from jax import lax
from jax.experimental import pallas as pl
from jax.experimental.pallas import tpu as pltpu
from jax.sharding import Mesh, PartitionSpec as P

logit_scale = 30.0
logit_bias = -5.0
epsilon = 1e-06

AXES = ("xh", "y", "core", "xl", "z")
SIZES = (2, 8, 2, 2, 8)
ALL = P(AXES, None)
SWAP = [(0, 1), (1, 0)]
LINE = 8
P_ORDER = (0, 4, 2, 6, 3, 7, 1, 5)
Q_ORDER = (0, 2, 4, 6, 1, 3, 5, 7)

IN_VMEM = pl.BlockSpec(memory_space=pltpu.VMEM)
IN_HBM = pl.BlockSpec(memory_space=pltpu.HBM)
IN_ANY = pl.BlockSpec(memory_space=pl.ANY)
IN_SMEM = pl.BlockSpec(memory_space=pltpu.SMEM)
PARAMS = pltpu.CompilerParams(vmem_limit_bytes=16 * 2**20)


def index_of(xh, y, core, xl, z):
    return (((xh * 8 + y) * 2 + core) * 2 + xl) * 8 + z


def line_groups(role, order):
    groups = []
    for core in range(2):
        for xh in range(2):
            for xl in range(2):
                for at in range(8):
                    if role(core) == 0:
                        groups.append([index_of(xh, at, core, xl, z) for z in order])
                    else:
                        groups.append([index_of(xh, y, core, xl, at) for y in order])
    return groups


def across_x(role):
    pairs = []
    for xh in range(2):
        for y in range(8):
            for core in range(2):
                for xl in range(2):
                    for z in range(8):
                        to = (xh ^ role(core), y, core, 1 - xl, z)
                        pairs.append((index_of(xh, y, core, xl, z), index_of(*to)))
    return pairs


def unit_rows(raw):
    wide = raw.astype(jnp.float32)
    inverse = lax.rsqrt(jnp.sum(wide * wide, axis=1, keepdims=True) + epsilon)
    return (wide * inverse, inverse)


def raw_grad(unit_sum, raw):
    unit, inverse = unit_rows(raw)
    along = jnp.sum(unit_sum * unit, axis=1, keepdims=True)
    return inverse * (unit_sum - along * unit)


def run_all(copies):
    for copy in copies:
        copy.start()
    for copy in copies:
        copy.wait()


def open_kernel(
    core_ref, images_hbm, texts_hbm, copies_ref, second_ref, images_ref, texts_ref, unit_ref, sems
):
    first = core_ref[0] == 0
    run_all(
        [
            pltpu.make_async_copy(images_hbm, images_ref, sems.at[0]),
            pltpu.make_async_copy(texts_hbm, texts_ref, sems.at[1]),
        ]
    )
    p_raw = jnp.where(first, images_ref[...], texts_ref[...])
    q_raw = jnp.where(first, texts_ref[...], images_ref[...])
    unit_ref[...] = unit_rows(p_raw)[0].astype(jnp.bfloat16)
    stores = [
        pltpu.make_async_copy(unit_ref, copies_ref.at[at], sems.at[at]) for at in range(LINE)
    ]
    for store in stores:
        store.start()
    second_ref[...] = unit_rows(q_raw)[0].astype(jnp.bfloat16)
    for store in stores:
        store.wait()


def open_rows(core, images, texts):
    shape = images.shape
    return pl.pallas_call(
        open_kernel,
        out_shape=(
            pltpu.HBM((LINE, *shape), jnp.bfloat16),
            jax.ShapeDtypeStruct(shape, jnp.bfloat16),
        ),
        in_specs=[IN_SMEM, IN_HBM, IN_HBM],
        out_specs=(IN_HBM, IN_VMEM),
        scratch_shapes=[pltpu.VMEM(shape, jnp.bfloat16)] * 3 + [pltpu.SemaphoreType.DMA((LINE,))],
        compiler_params=PARAMS,
    )(core, images, texts)


def copies_kernel(near_ref, far_ref, out_ref, sems):
    rows = near_ref.shape[0]
    copies = []
    for at in range(LINE):
        for half, ref in enumerate((near_ref, far_ref)):
            target = out_ref.at[at, pl.ds(half * rows, rows)]
            copies.append(pltpu.make_async_copy(ref, target, sems.at[2 * at + half]))
    run_all(copies)


def copies(near, far):
    rows, width = near.shape
    return pl.pallas_call(
        copies_kernel,
        out_shape=pltpu.HBM((LINE, 2 * rows, width), near.dtype),
        in_specs=[IN_VMEM, IN_VMEM],
        out_specs=IN_HBM,
        scratch_shapes=[pltpu.SemaphoreType.DMA((2 * LINE,))],
        compiler_params=PARAMS,
    )(near, far)


def hold_kernel(*refs):
    del refs


def hold(kept, after):
    return pl.pallas_call(
        hold_kernel,
        out_shape=jax.ShapeDtypeStruct(kept.shape, kept.dtype),
        in_specs=[IN_ANY] * (1 + len(after)),
        out_specs=IN_ANY,
        input_output_aliases={0: 0},
        compiler_params=PARAMS,
    )(kept, *after)


def block_of(ref, half):
    if half is not None:
        rows = ref.shape[1] // 2
        value = ref[:, half * rows : (half + 1) * rows, :]
    else:
        value = ref[...]
    return value.reshape(-1, value.shape[-1])


def pull_kernel(halves, parts, loads, labelled, added, waits, kind, *refs):
    refs = list(refs)
    at_ref = refs.pop(0) if labelled else None
    mine = [(refs.pop(0), half) for half in halves]
    theirs = [refs.pop(0) for _ in range(parts)]
    so_far_ref = refs.pop(0) if added else None
    if waits:
        refs.pop(0)
    out_ref = refs.pop(0)
    load = None
    if loads:
        loaded_ref, load_sem = refs.pop(0), refs.pop(0)
        load = pltpu.make_async_copy(theirs[-1], loaded_ref, load_sem)
        load.start()
        theirs[-1] = loaded_ref
    stores = []
    for block, (ref, half) in enumerate(mine):
        rows = block_of(ref, half)
        total = None
        for part, theirs_ref in enumerate(theirs):
            if load is not None and part == parts - 1:
                load.wait()
                load = None
            scores = lax.dot_general(
                rows,
                block_of(theirs_ref, None),
                (((1,), (1,)), ((), ())),
                preferred_element_type=jnp.float32,
            )
            chance = 1.0 / (1.0 + jnp.exp(-logit_bias - logit_scale * scores))
            if labelled == (block, part):
                row = lax.broadcasted_iota(jnp.int32, scores.shape, 0) - at_ref[0]
                column = lax.broadcasted_iota(jnp.int32, scores.shape, 1) - at_ref[1]
                same = (row == column) & (row >= 0) & (row < at_ref[2])
                chance = jnp.where(same, chance - 1.0, chance)
            coef = (logit_scale * chance).astype(jnp.bfloat16)
            if kind == "line" and part == parts - 1:
                break
            terms = jnp.dot(coef, block_of(theirs_ref, None), preferred_element_type=jnp.float32)
            total = terms if total is None else total + terms
        size = rows.shape[0]
        if kind == "vmem":
            if added:
                total = total + so_far_ref[block * size : (block + 1) * size].astype(jnp.float32)
            out_ref[block * size : (block + 1) * size] = total.astype(out_ref.dtype)
            continue
        stage_ref, sems = refs
        for half, (start, end) in enumerate(((0, size // 2), (size // 2, 3 * size // 4), (3 * size // 4, size))):
            rows = slice(start, end)
            terms = jnp.dot(
                coef[rows], block_of(theirs[-1], None), preferred_element_type=jnp.float32
            )
            if total is not None:
                terms = terms + total[rows]
            if added:
                terms = terms + so_far_ref[rows].astype(jnp.float32)
            stage_ref[rows] = terms.astype(stage_ref.dtype)
            stores.append(
                pltpu.make_async_copy(stage_ref.at[rows], out_ref.at[rows], sems.at[half])
            )
            stores[-1].start()
    for store in stores:
        store.wait()


def pull(
    mine,
    theirs,
    at=None,
    labelled=None,
    so_far=None,
    after=None,
    load=False,
    kind="vmem",
    dtype=jnp.float32,
):
    halves = [half for _, half in mine]
    width = theirs[0].shape[-1]
    size = sum(part.size for part in theirs) // width
    rows = [part.size // width // (1 if half is None else 2) for part, half in mine]
    args = [part for part, _ in mine] + list(theirs)
    specs = [IN_VMEM] * len(args)
    if load:
        specs[-1] = IN_HBM
    if labelled:
        args.insert(0, at)
        specs.insert(0, IN_SMEM)
    if so_far is not None:
        args.append(so_far)
        specs.append(IN_VMEM)
    if after is not None:
        args.append(after)
        specs.append(IN_ANY)
    shape, scratch = (sum(rows), width), []
    if load:
        scratch += [pltpu.VMEM(theirs[-1].shape, jnp.bfloat16), pltpu.SemaphoreType.DMA(())]
    if kind == "line":
        scratch += [pltpu.VMEM(shape, dtype), pltpu.SemaphoreType.DMA((3,))]
    return pl.pallas_call(
        functools.partial(
            pull_kernel,
            halves,
            len(theirs),
            load,
            labelled,
            so_far is not None,
            after is not None,
            kind,
        ),
        out_shape=(jax.ShapeDtypeStruct if kind == "vmem" else pltpu.HBM)(shape, dtype),
        in_specs=specs,
        out_specs=IN_VMEM if kind == "vmem" else IN_HBM,
        scratch_shapes=scratch,
        compiler_params=PARAMS,
        cost_estimate=pl.CostEstimate(
            flops=4 * sum(rows) * size * width,
            bytes_accessed=8 * sum(rows) * width,
            transcendentals=2 * sum(rows) * size,
        ),
    )(*args)


def add_kernel(one_ref, two_ref, out_ref, stage_ref, sem):
    total = (one_ref[...] + two_ref[...].astype(jnp.float32)).astype(jnp.bfloat16)
    stage_ref[...] = total.reshape(stage_ref.shape)
    run_all([pltpu.make_async_copy(stage_ref, out_ref, sem)])


def add_rows(one, two):
    shape = (LINE, one.shape[0] // LINE, one.shape[1])
    return pl.pallas_call(
        add_kernel,
        out_shape=pltpu.HBM(shape, jnp.bfloat16),
        in_specs=[IN_VMEM, IN_VMEM],
        out_specs=IN_HBM,
        scratch_shapes=[pltpu.VMEM(shape, jnp.bfloat16), pltpu.SemaphoreType.DMA(())],
        compiler_params=PARAMS,
    )(one, two)


def line_sum(back_ref, start, rows):
    total = back_ref[0, start : start + rows].astype(jnp.float32)
    for place in range(1, LINE):
        total = total + back_ref[place, start : start + rows].astype(jnp.float32)
    return total


def sum_kernel(back_ref, near_ref, far_ref):
    rows = near_ref.shape[0]
    near_ref[...] = line_sum(back_ref, 0, rows)
    far_ref[...] = line_sum(back_ref, rows, rows).astype(far_ref.dtype)


def sum_rows(back):
    shape = (back.shape[1] // 2, back.shape[2])
    return pl.pallas_call(
        sum_kernel,
        out_shape=(
            jax.ShapeDtypeStruct(shape, jnp.float32),
            jax.ShapeDtypeStruct(shape, jnp.bfloat16),
        ),
        in_specs=[IN_VMEM],
        out_specs=(IN_VMEM, IN_VMEM),
        compiler_params=PARAMS,
    )(back)


def close_kernel(core_ref, near_ref, far_ref, back_ref, images_ref, texts_ref, img_ref, txt_ref):
    first = core_ref[0] == 0
    q_sum = near_ref[...] + far_ref[...].astype(jnp.float32)
    p_sum = line_sum(back_ref, 0, near_ref.shape[0])
    img_ref[...] = raw_grad(jnp.where(first, p_sum, q_sum), images_ref[...])
    txt_ref[...] = raw_grad(jnp.where(first, q_sum, p_sum), texts_ref[...])


def close_rows(core, near, far, back, images, texts):
    shape = jax.ShapeDtypeStruct(near.shape, jnp.float32)
    return pl.pallas_call(
        close_kernel,
        out_shape=(shape, shape),
        in_specs=[IN_SMEM] + [IN_VMEM] * 5,
        out_specs=(IN_VMEM, IN_VMEM),
        compiler_params=PARAMS,
    )(core, near, far, back, images, texts)


def in_hbm(array):
    return pltpu.with_memory_space_constraint(array, pltpu.HBM)


def in_vmem(array):
    return pltpu.with_memory_space_constraint(array, pltpu.VMEM)


def trade(blocks, role, order):
    groups = line_groups(role, order)
    return lax.all_to_all(
        blocks, AXES, split_axis=0, concat_axis=0, axis_index_groups=groups, tiled=True
    )


def place_in(order, at):
    return sum(jnp.where(at == where, place, 0) for place, where in enumerate(order))


def swap_x(block, role):
    return lax.ppermute(block, AXES, across_x(role))


def p_role(core):
    return core


def q_role(core):
    return 1 - core


def local(images, texts):
    rows, width = images.shape
    bf = jnp.bfloat16
    core = lax.axis_index("core")
    y, z = lax.axis_index("y"), lax.axis_index("z")
    p_place = place_in(P_ORDER, jnp.where(core == 0, z, y))
    q_place = place_in(Q_ORDER, jnp.where(core == 0, y, z))
    core = core.astype(jnp.int32).reshape(1)

    copies_p, own_q = open_rows(core, in_hbm(images), in_hbm(texts))
    near_p = trade(copies_p, p_role, P_ORDER).reshape(-1, width)
    copies_q = copies(own_q, swap_x(own_q, q_role))
    near_p = hold(near_p, [in_hbm(copies_q)])
    mine_q = trade(copies_q, q_role, Q_ORDER)
    far_p = swap_x(near_p, p_role)
    theirs_p = in_hbm(lax.ppermute(jnp.concatenate([near_p, far_p], 0), "core", SWAP))

    at_pq = jnp.stack([p_place * rows, q_place * 2 * rows, rows]).astype(jnp.int32)
    at_qp = jnp.stack([q_place * 2 * rows, p_place * rows, rows]).astype(jnp.int32)
    all_q = [(mine_q, None)]
    theirs_q = in_vmem(lax.ppermute(mine_q.reshape(-1, width), "core", SWAP))
    sum_q = pull(all_q, [near_p, far_p], at=at_qp, labelled=(0, 0), after=theirs_p, dtype=bf)
    sum_q = pull(all_q, [theirs_q], so_far=sum_q, kind="line", dtype=bf)
    near, far = sum_rows(trade(sum_q.reshape(mine_q.shape), q_role, Q_ORDER))
    far = swap_x(far, q_role)

    others = [mine_q, theirs_p]
    back_p = swap_x(pull([(far_p, None)], others, load=True, dtype=bf), p_role)
    near_p = pull([(near_p, None)], others, at=at_pq, labelled=(0, 0), load=True)
    back_p = trade(add_rows(near_p, back_p), p_role, P_ORDER)
    return close_rows(core, near, far, back_p, images, texts)


def solution(mesh):
    fine = Mesh(mesh.devices.reshape(SIZES), AXES)
    return jax.shard_map(
        local, mesh=fine, in_specs=(ALL, ALL), out_specs=(ALL, ALL), check_vma=False
    )
```

```python
import functools

import jax
import jax.numpy as jnp
from jax import lax
from jax.experimental import pallas as pl
from jax.experimental.pallas import tpu as pltpu
from jax.sharding import Mesh, PartitionSpec as P

logit_scale = 30.0
logit_bias = -5.0
epsilon = 1e-06

AXES = ("xh", "y", "core", "xl", "z")
SIZES = (2, 8, 2, 2, 8)
ALL = P(AXES, None)
SWAP = [(0, 1), (1, 0)]
LINE = 8
P_ORDER = (0, 4, 2, 6, 3, 7, 1, 5)
Q_ORDER = (0, 2, 4, 6, 1, 3, 5, 7)

IN_VMEM = pl.BlockSpec(memory_space=pltpu.VMEM)
IN_HBM = pl.BlockSpec(memory_space=pltpu.HBM)
IN_ANY = pl.BlockSpec(memory_space=pl.ANY)
IN_SMEM = pl.BlockSpec(memory_space=pltpu.SMEM)
PARAMS = pltpu.CompilerParams(vmem_limit_bytes=16 * 2**20)


def index_of(xh, y, core, xl, z):
    return (((xh * 8 + y) * 2 + core) * 2 + xl) * 8 + z


def line_groups(role, order):
    groups = []
    for core in range(2):
        for xh in range(2):
            for xl in range(2):
                for at in range(8):
                    if role(core) == 0:
                        groups.append([index_of(xh, at, core, xl, z) for z in order])
                    else:
                        groups.append([index_of(xh, y, core, xl, at) for y in order])
    return groups


def across_x(role):
    pairs = []
    for xh in range(2):
        for y in range(8):
            for core in range(2):
                for xl in range(2):
                    for z in range(8):
                        to = (xh ^ role(core), y, core, 1 - xl, z)
                        pairs.append((index_of(xh, y, core, xl, z), index_of(*to)))
    return pairs


def unit_rows(raw):
    wide = raw.astype(jnp.float32)
    inverse = lax.rsqrt(jnp.sum(wide * wide, axis=1, keepdims=True) + epsilon)
    return (wide * inverse, inverse)


def raw_grad(unit_sum, raw):
    unit, inverse = unit_rows(raw)
    along = jnp.sum(unit_sum * unit, axis=1, keepdims=True)
    return inverse * (unit_sum - along * unit)


def run_all(copies):
    for copy in copies:
        copy.start()
    for copy in copies:
        copy.wait()


def open_kernel(
    core_ref, images_hbm, texts_hbm, copies_ref, second_ref, images_ref, texts_ref, unit_ref, sems
):
    first = core_ref[0] == 0
    run_all(
        [
            pltpu.make_async_copy(images_hbm, images_ref, sems.at[0]),
            pltpu.make_async_copy(texts_hbm, texts_ref, sems.at[1]),
        ]
    )
    p_raw = jnp.where(first, images_ref[...], texts_ref[...])
    q_raw = jnp.where(first, texts_ref[...], images_ref[...])
    unit_ref[...] = unit_rows(p_raw)[0].astype(jnp.bfloat16)
    stores = [
        pltpu.make_async_copy(unit_ref, copies_ref.at[at], sems.at[at]) for at in range(LINE)
    ]
    for store in stores:
        store.start()
    second_ref[...] = unit_rows(q_raw)[0].astype(jnp.bfloat16)
    for store in stores:
        store.wait()


def open_rows(core, images, texts):
    shape = images.shape
    return pl.pallas_call(
        open_kernel,
        out_shape=(
            pltpu.HBM((LINE, *shape), jnp.bfloat16),
            jax.ShapeDtypeStruct(shape, jnp.bfloat16),
        ),
        in_specs=[IN_SMEM, IN_HBM, IN_HBM],
        out_specs=(IN_HBM, IN_VMEM),
        scratch_shapes=[pltpu.VMEM(shape, jnp.bfloat16)] * 3 + [pltpu.SemaphoreType.DMA((LINE,))],
        compiler_params=PARAMS,
    )(core, images, texts)


def copies_kernel(near_ref, far_ref, out_ref, sems):
    rows = near_ref.shape[0]
    copies = []
    for at in range(LINE):
        for half, ref in enumerate((near_ref, far_ref)):
            target = out_ref.at[at, pl.ds(half * rows, rows)]
            copies.append(pltpu.make_async_copy(ref, target, sems.at[2 * at + half]))
    run_all(copies)


def copies(near, far):
    rows, width = near.shape
    return pl.pallas_call(
        copies_kernel,
        out_shape=pltpu.HBM((LINE, 2 * rows, width), near.dtype),
        in_specs=[IN_VMEM, IN_VMEM],
        out_specs=IN_HBM,
        scratch_shapes=[pltpu.SemaphoreType.DMA((2 * LINE,))],
        compiler_params=PARAMS,
    )(near, far)


def hold_kernel(*refs):
    del refs


def hold(kept, after):
    return pl.pallas_call(
        hold_kernel,
        out_shape=jax.ShapeDtypeStruct(kept.shape, kept.dtype),
        in_specs=[IN_ANY] * (1 + len(after)),
        out_specs=IN_ANY,
        input_output_aliases={0: 0},
        compiler_params=PARAMS,
    )(kept, *after)


def block_of(ref, half):
    if half is not None:
        rows = ref.shape[1] // 2
        value = ref[:, half * rows : (half + 1) * rows, :]
    else:
        value = ref[...]
    return value.reshape(-1, value.shape[-1])


def pull_kernel(halves, parts, loads, labelled, added, waits, kind, *refs):
    refs = list(refs)
    at_ref = refs.pop(0) if labelled else None
    mine = [(refs.pop(0), half) for half in halves]
    theirs = [refs.pop(0) for _ in range(parts)]
    so_far_ref = refs.pop(0) if added else None
    if waits:
        refs.pop(0)
    out_ref = refs.pop(0)
    load = None
    if loads:
        loaded_ref, load_sem = refs.pop(0), refs.pop(0)
        load = pltpu.make_async_copy(theirs[-1], loaded_ref, load_sem)
        load.start()
        theirs[-1] = loaded_ref
    stores = []
    for block, (ref, half) in enumerate(mine):
        rows = block_of(ref, half)
        total = None
        for part, theirs_ref in enumerate(theirs):
            if load is not None and part == parts - 1:
                load.wait()
                load = None
            scores = lax.dot_general(
                rows,
                block_of(theirs_ref, None),
                (((1,), (1,)), ((), ())),
                preferred_element_type=jnp.float32,
            )
            chance = 1.0 / (1.0 + jnp.exp(-logit_bias - logit_scale * scores))
            if labelled == (block, part):
                row = lax.broadcasted_iota(jnp.int32, scores.shape, 0) - at_ref[0]
                column = lax.broadcasted_iota(jnp.int32, scores.shape, 1) - at_ref[1]
                same = (row == column) & (row >= 0) & (row < at_ref[2])
                chance = jnp.where(same, chance - 1.0, chance)
            coef = (logit_scale * chance).astype(jnp.bfloat16)
            if kind == "line" and part == parts - 1:
                break
            terms = jnp.dot(coef, block_of(theirs_ref, None), preferred_element_type=jnp.float32)
            total = terms if total is None else total + terms
        size = rows.shape[0]
        if kind == "vmem":
            if added:
                total = total + so_far_ref[block * size : (block + 1) * size].astype(jnp.float32)
            out_ref[block * size : (block + 1) * size] = total.astype(out_ref.dtype)
            continue
        stage_ref, sems = refs
        for half in range(2):
            rows = slice(half * size // 2, (half + 1) * size // 2)
            terms = jnp.dot(
                coef[rows], block_of(theirs[-1], None), preferred_element_type=jnp.float32
            )
            if total is not None:
                terms = terms + total[rows]
            if added:
                terms = terms + so_far_ref[rows].astype(jnp.float32)
            stage_ref[rows] = terms.astype(stage_ref.dtype)
            stores.append(
                pltpu.make_async_copy(stage_ref.at[rows], out_ref.at[rows], sems.at[half])
            )
            stores[-1].start()
    for store in stores:
        store.wait()


def pull(
    mine,
    theirs,
    at=None,
    labelled=None,
    so_far=None,
    after=None,
    load=False,
    kind="vmem",
    dtype=jnp.float32,
):
    halves = [half for _, half in mine]
    width = theirs[0].shape[-1]
    size = sum(part.size for part in theirs) // width
    rows = [part.size // width // (1 if half is None else 2) for part, half in mine]
    args = [part for part, _ in mine] + list(theirs)
    specs = [IN_VMEM] * len(args)
    if load:
        specs[-1] = IN_HBM
    if labelled:
        args.insert(0, at)
        specs.insert(0, IN_SMEM)
    if so_far is not None:
        args.append(so_far)
        specs.append(IN_VMEM)
    if after is not None:
        args.append(after)
        specs.append(IN_ANY)
    shape, scratch = (sum(rows), width), []
    if load:
        scratch += [pltpu.VMEM(theirs[-1].shape, jnp.bfloat16), pltpu.SemaphoreType.DMA(())]
    if kind == "line":
        scratch += [pltpu.VMEM(shape, dtype), pltpu.SemaphoreType.DMA((2,))]
    return pl.pallas_call(
        functools.partial(
            pull_kernel,
            halves,
            len(theirs),
            load,
            labelled,
            so_far is not None,
            after is not None,
            kind,
        ),
        out_shape=(jax.ShapeDtypeStruct if kind == "vmem" else pltpu.HBM)(shape, dtype),
        in_specs=specs,
        out_specs=IN_VMEM if kind == "vmem" else IN_HBM,
        scratch_shapes=scratch,
        compiler_params=PARAMS,
        cost_estimate=pl.CostEstimate(
            flops=4 * sum(rows) * size * width,
            bytes_accessed=8 * sum(rows) * width,
            transcendentals=2 * sum(rows) * size,
        ),
    )(*args)


def add_kernel(one_ref, two_ref, out_ref, stage_ref, sem):
    total = (one_ref[...] + two_ref[...].astype(jnp.float32)).astype(jnp.bfloat16)
    stage_ref[...] = total.reshape(stage_ref.shape)
    run_all([pltpu.make_async_copy(stage_ref, out_ref, sem)])


def add_rows(one, two):
    shape = (LINE, one.shape[0] // LINE, one.shape[1])
    return pl.pallas_call(
        add_kernel,
        out_shape=pltpu.HBM(shape, jnp.bfloat16),
        in_specs=[IN_VMEM, IN_VMEM],
        out_specs=IN_HBM,
        scratch_shapes=[pltpu.VMEM(shape, jnp.bfloat16), pltpu.SemaphoreType.DMA(())],
        compiler_params=PARAMS,
    )(one, two)


def line_sum(back_ref, start, rows):
    total = back_ref[0, start : start + rows].astype(jnp.float32)
    for place in range(1, LINE):
        total = total + back_ref[place, start : start + rows].astype(jnp.float32)
    return total


def sum_kernel(back_ref, near_ref, far_ref):
    rows = near_ref.shape[0]
    near_ref[...] = line_sum(back_ref, 0, rows)
    far_ref[...] = line_sum(back_ref, rows, rows).astype(far_ref.dtype)


def sum_rows(back):
    shape = (back.shape[1] // 2, back.shape[2])
    return pl.pallas_call(
        sum_kernel,
        out_shape=(
            jax.ShapeDtypeStruct(shape, jnp.float32),
            jax.ShapeDtypeStruct(shape, jnp.bfloat16),
        ),
        in_specs=[IN_VMEM],
        out_specs=(IN_VMEM, IN_VMEM),
        compiler_params=PARAMS,
    )(back)


def q_grad_kernel(core_ref, near_ref, far_ref, images_ref, texts_ref, out_ref):
    raw = jnp.where(core_ref[0] == 0, texts_ref[...], images_ref[...])
    out_ref[...] = raw_grad(near_ref[...] + far_ref[...].astype(jnp.float32), raw)


def q_grad(core, near, far, images, texts):
    return pl.pallas_call(
        q_grad_kernel,
        out_shape=jax.ShapeDtypeStruct(near.shape, jnp.float32),
        in_specs=[IN_SMEM] + [IN_VMEM] * 4,
        out_specs=IN_VMEM,
        compiler_params=PARAMS,
    )(core, near, far, images, texts)


def close_kernel(core_ref, q_ref, back_ref, images_ref, texts_ref, img_ref, txt_ref):
    first = core_ref[0] == 0
    raw = jnp.where(first, images_ref[...], texts_ref[...])
    grad = raw_grad(line_sum(back_ref, 0, q_ref.shape[0]), raw)
    img_ref[...] = jnp.where(first, grad, q_ref[...])
    txt_ref[...] = jnp.where(first, q_ref[...], grad)


def close_rows(core, q, back, images, texts):
    shape = jax.ShapeDtypeStruct(q.shape, jnp.float32)
    return pl.pallas_call(
        close_kernel,
        out_shape=(shape, shape),
        in_specs=[IN_SMEM] + [IN_VMEM] * 4,
        out_specs=(IN_VMEM, IN_VMEM),
        compiler_params=PARAMS,
    )(core, q, back, images, texts)


def in_hbm(array):
    return pltpu.with_memory_space_constraint(array, pltpu.HBM)


def in_vmem(array):
    return pltpu.with_memory_space_constraint(array, pltpu.VMEM)


def trade(blocks, role, order):
    groups = line_groups(role, order)
    return lax.all_to_all(
        blocks, AXES, split_axis=0, concat_axis=0, axis_index_groups=groups, tiled=True
    )


def place_in(order, at):
    return sum(jnp.where(at == where, place, 0) for place, where in enumerate(order))


def swap_x(block, role):
    return lax.ppermute(block, AXES, across_x(role))


def p_role(core):
    return core


def q_role(core):
    return 1 - core


def local(images, texts):
    rows, width = images.shape
    bf = jnp.bfloat16
    core = lax.axis_index("core")
    y, z = lax.axis_index("y"), lax.axis_index("z")
    p_place = place_in(P_ORDER, jnp.where(core == 0, z, y))
    q_place = place_in(Q_ORDER, jnp.where(core == 0, y, z))
    core = core.astype(jnp.int32).reshape(1)

    copies_p, own_q = open_rows(core, in_hbm(images), in_hbm(texts))
    near_p = trade(copies_p, p_role, P_ORDER).reshape(-1, width)
    copies_q = copies(own_q, swap_x(own_q, q_role))
    near_p = hold(near_p, [in_hbm(copies_q)])
    mine_q = trade(copies_q, q_role, Q_ORDER)
    far_p = swap_x(near_p, p_role)
    theirs_p = in_hbm(lax.ppermute(jnp.concatenate([near_p, far_p], 0), "core", SWAP))

    at_pq = jnp.stack([p_place * rows, q_place * 2 * rows, rows]).astype(jnp.int32)
    at_qp = jnp.stack([q_place * 2 * rows, p_place * rows, rows]).astype(jnp.int32)
    all_q = [(mine_q, None)]
    theirs_q = in_vmem(lax.ppermute(mine_q.reshape(-1, width), "core", SWAP))
    sum_q = pull(all_q, [near_p, far_p], at=at_qp, labelled=(0, 0), after=theirs_p, dtype=bf)
    sum_q = pull(all_q, [theirs_q], so_far=sum_q, kind="line", dtype=bf)
    near, far = sum_rows(trade(sum_q.reshape(mine_q.shape), q_role, Q_ORDER))
    far = swap_x(far, q_role)

    others = [mine_q, theirs_p]
    back_p = swap_x(pull([(far_p, None)], others, load=True, dtype=bf), p_role)
    near_p = pull([(near_p, None)], others, at=at_pq, labelled=(0, 0), load=True)
    back_p = trade(add_rows(near_p, back_p), p_role, P_ORDER)
    q = q_grad(core, near, far, images, texts)
    return close_rows(core, q, back_p, images, texts)


def solution(mesh):
    fine = Mesh(mesh.devices.reshape(SIZES), AXES)
    return jax.shard_map(
        local, mesh=fine, in_specs=(ALL, ALL), out_specs=(ALL, ALL), check_vma=False
    )
```

```python
import functools

import jax
import jax.numpy as jnp
from jax import lax
from jax.experimental import pallas as pl
from jax.experimental.pallas import tpu as pltpu
from jax.sharding import Mesh, PartitionSpec as P

logit_scale = 30.0
logit_bias = -5.0
epsilon = 1e-06

AXES = ("xh", "y", "core", "xl", "z")
SIZES = (2, 8, 2, 2, 8)
ALL = P(AXES, None)
SWAP = [(0, 1), (1, 0)]
LINE = 8
P_ORDER = (0, 2, 4, 6, 1, 3, 5, 7)
Q_ORDER = (0, 2, 4, 6, 1, 3, 5, 7)

IN_VMEM = pl.BlockSpec(memory_space=pltpu.VMEM)
IN_HBM = pl.BlockSpec(memory_space=pltpu.HBM)
IN_ANY = pl.BlockSpec(memory_space=pl.ANY)
IN_SMEM = pl.BlockSpec(memory_space=pltpu.SMEM)
PARAMS = pltpu.CompilerParams(vmem_limit_bytes=16 * 2**20)


def index_of(xh, y, core, xl, z):
    return (((xh * 8 + y) * 2 + core) * 2 + xl) * 8 + z


def line_groups(role, order):
    groups = []
    for core in range(2):
        for xh in range(2):
            for xl in range(2):
                for at in range(8):
                    if role(core) == 0:
                        groups.append([index_of(xh, at, core, xl, z) for z in order])
                    else:
                        groups.append([index_of(xh, y, core, xl, at) for y in order])
    return groups


def across_x(role):
    pairs = []
    for xh in range(2):
        for y in range(8):
            for core in range(2):
                for xl in range(2):
                    for z in range(8):
                        to = (xh ^ role(core), y, core, 1 - xl, z)
                        pairs.append((index_of(xh, y, core, xl, z), index_of(*to)))
    return pairs


def unit_rows(raw):
    wide = raw.astype(jnp.float32)
    inverse = lax.rsqrt(jnp.sum(wide * wide, axis=1, keepdims=True) + epsilon)
    return (wide * inverse, inverse)


def raw_grad(unit_sum, raw):
    unit, inverse = unit_rows(raw)
    along = jnp.sum(unit_sum * unit, axis=1, keepdims=True)
    return inverse * (unit_sum - along * unit)


def run_all(copies):
    for copy in copies:
        copy.start()
    for copy in copies:
        copy.wait()


def open_kernel(
    core_ref, images_hbm, texts_hbm, copies_ref, second_ref, images_ref, texts_ref, unit_ref, sems
):
    first = core_ref[0] == 0
    run_all(
        [
            pltpu.make_async_copy(images_hbm, images_ref, sems.at[0]),
            pltpu.make_async_copy(texts_hbm, texts_ref, sems.at[1]),
        ]
    )
    p_raw = jnp.where(first, images_ref[...], texts_ref[...])
    q_raw = jnp.where(first, texts_ref[...], images_ref[...])
    unit_ref[...] = unit_rows(p_raw)[0].astype(jnp.bfloat16)
    stores = [
        pltpu.make_async_copy(unit_ref, copies_ref.at[at], sems.at[at]) for at in range(LINE)
    ]
    for store in stores:
        store.start()
    second_ref[...] = unit_rows(q_raw)[0].astype(jnp.bfloat16)
    for store in stores:
        store.wait()


def open_rows(core, images, texts):
    shape = images.shape
    return pl.pallas_call(
        open_kernel,
        out_shape=(
            pltpu.HBM((LINE, *shape), jnp.bfloat16),
            jax.ShapeDtypeStruct(shape, jnp.bfloat16),
        ),
        in_specs=[IN_SMEM, IN_HBM, IN_HBM],
        out_specs=(IN_HBM, IN_VMEM),
        scratch_shapes=[pltpu.VMEM(shape, jnp.bfloat16)] * 3 + [pltpu.SemaphoreType.DMA((LINE,))],
        compiler_params=PARAMS,
    )(core, images, texts)


def copies_kernel(near_ref, far_ref, out_ref, sems):
    rows = near_ref.shape[0]
    copies = []
    for at in range(LINE):
        for half, ref in enumerate((near_ref, far_ref)):
            target = out_ref.at[at, pl.ds(half * rows, rows)]
            copies.append(pltpu.make_async_copy(ref, target, sems.at[2 * at + half]))
    run_all(copies)


def copies(near, far):
    rows, width = near.shape
    return pl.pallas_call(
        copies_kernel,
        out_shape=pltpu.HBM((LINE, 2 * rows, width), near.dtype),
        in_specs=[IN_VMEM, IN_VMEM],
        out_specs=IN_HBM,
        scratch_shapes=[pltpu.SemaphoreType.DMA((2 * LINE,))],
        compiler_params=PARAMS,
    )(near, far)


def hold_kernel(*refs):
    del refs


def hold(kept, after):
    return pl.pallas_call(
        hold_kernel,
        out_shape=jax.ShapeDtypeStruct(kept.shape, kept.dtype),
        in_specs=[IN_ANY] * (1 + len(after)),
        out_specs=IN_ANY,
        input_output_aliases={0: 0},
        compiler_params=PARAMS,
    )(kept, *after)


def block_of(ref, half):
    if half is not None:
        rows = ref.shape[1] // 2
        value = ref[:, half * rows : (half + 1) * rows, :]
    else:
        value = ref[...]
    return value.reshape(-1, value.shape[-1])


def pull_kernel(halves, parts, loads, labelled, added, waits, kind, *refs):
    refs = list(refs)
    at_ref = refs.pop(0) if labelled else None
    mine = [(refs.pop(0), half) for half in halves]
    theirs = [refs.pop(0) for _ in range(parts)]
    so_far_ref = refs.pop(0) if added else None
    if waits:
        refs.pop(0)
    out_ref = refs.pop(0)
    load = None
    if loads:
        loaded_ref, load_sem = refs.pop(0), refs.pop(0)
        load = pltpu.make_async_copy(theirs[-1], loaded_ref, load_sem)
        load.start()
        theirs[-1] = loaded_ref
    stores = []
    for block, (ref, half) in enumerate(mine):
        rows = block_of(ref, half)
        total = None
        for part, theirs_ref in enumerate(theirs):
            if load is not None and part == parts - 1:
                load.wait()
                load = None
            scores = lax.dot_general(
                rows,
                block_of(theirs_ref, None),
                (((1,), (1,)), ((), ())),
                preferred_element_type=jnp.float32,
            )
            chance = 1.0 / (1.0 + jnp.exp(-logit_bias - logit_scale * scores))
            if labelled == (block, part):
                row = lax.broadcasted_iota(jnp.int32, scores.shape, 0) - at_ref[0]
                column = lax.broadcasted_iota(jnp.int32, scores.shape, 1) - at_ref[1]
                same = (row == column) & (row >= 0) & (row < at_ref[2])
                chance = jnp.where(same, chance - 1.0, chance)
            coef = (logit_scale * chance).astype(jnp.bfloat16)
            if kind == "line" and part == parts - 1:
                break
            terms = jnp.dot(coef, block_of(theirs_ref, None), preferred_element_type=jnp.float32)
            total = terms if total is None else total + terms
        size = rows.shape[0]
        if kind == "vmem":
            if added:
                total = total + so_far_ref[block * size : (block + 1) * size].astype(jnp.float32)
            out_ref[block * size : (block + 1) * size] = total.astype(out_ref.dtype)
            continue
        stage_ref, sems = refs
        for half in range(2):
            rows = slice(half * size // 2, (half + 1) * size // 2)
            terms = jnp.dot(
                coef[rows], block_of(theirs[-1], None), preferred_element_type=jnp.float32
            )
            if total is not None:
                terms = terms + total[rows]
            if added:
                terms = terms + so_far_ref[rows].astype(jnp.float32)
            stage_ref[rows] = terms.astype(stage_ref.dtype)
            stores.append(
                pltpu.make_async_copy(stage_ref.at[rows], out_ref.at[rows], sems.at[half])
            )
            stores[-1].start()
    for store in stores:
        store.wait()


def pull(
    mine,
    theirs,
    at=None,
    labelled=None,
    so_far=None,
    after=None,
    load=False,
    kind="vmem",
    dtype=jnp.float32,
):
    halves = [half for _, half in mine]
    width = theirs[0].shape[-1]
    size = sum(part.size for part in theirs) // width
    rows = [part.size // width // (1 if half is None else 2) for part, half in mine]
    args = [part for part, _ in mine] + list(theirs)
    specs = [IN_VMEM] * len(args)
    if load:
        specs[-1] = IN_HBM
    if labelled:
        args.insert(0, at)
        specs.insert(0, IN_SMEM)
    if so_far is not None:
        args.append(so_far)
        specs.append(IN_VMEM)
    if after is not None:
        args.append(after)
        specs.append(IN_ANY)
    shape, scratch = (sum(rows), width), []
    if load:
        scratch += [pltpu.VMEM(theirs[-1].shape, jnp.bfloat16), pltpu.SemaphoreType.DMA(())]
    if kind == "line":
        scratch += [pltpu.VMEM(shape, dtype), pltpu.SemaphoreType.DMA((2,))]
    return pl.pallas_call(
        functools.partial(
            pull_kernel,
            halves,
            len(theirs),
            load,
            labelled,
            so_far is not None,
            after is not None,
            kind,
        ),
        out_shape=(jax.ShapeDtypeStruct if kind == "vmem" else pltpu.HBM)(shape, dtype),
        in_specs=specs,
        out_specs=IN_VMEM if kind == "vmem" else IN_HBM,
        scratch_shapes=scratch,
        compiler_params=PARAMS,
        cost_estimate=pl.CostEstimate(
            flops=4 * sum(rows) * size * width,
            bytes_accessed=8 * sum(rows) * width,
            transcendentals=2 * sum(rows) * size,
        ),
    )(*args)


def add_kernel(one_ref, two_ref, out_ref, stage_ref, sem):
    total = (one_ref[...] + two_ref[...].astype(jnp.float32)).astype(jnp.bfloat16)
    stage_ref[...] = total.reshape(stage_ref.shape)
    run_all([pltpu.make_async_copy(stage_ref, out_ref, sem)])


def add_rows(one, two):
    shape = (LINE, one.shape[0] // LINE, one.shape[1])
    return pl.pallas_call(
        add_kernel,
        out_shape=pltpu.HBM(shape, jnp.bfloat16),
        in_specs=[IN_VMEM, IN_VMEM],
        out_specs=IN_HBM,
        scratch_shapes=[pltpu.VMEM(shape, jnp.bfloat16), pltpu.SemaphoreType.DMA(())],
        compiler_params=PARAMS,
    )(one, two)


def line_sum(back_ref, start, rows):
    total = back_ref[0, start : start + rows].astype(jnp.float32)
    for place in range(1, LINE):
        total = total + back_ref[place, start : start + rows].astype(jnp.float32)
    return total


def sum_kernel(back_ref, near_ref, far_ref):
    rows = near_ref.shape[0]
    near_ref[...] = line_sum(back_ref, 0, rows)
    far_ref[...] = line_sum(back_ref, rows, rows).astype(far_ref.dtype)


def sum_rows(back):
    shape = (back.shape[1] // 2, back.shape[2])
    return pl.pallas_call(
        sum_kernel,
        out_shape=(
            jax.ShapeDtypeStruct(shape, jnp.float32),
            jax.ShapeDtypeStruct(shape, jnp.bfloat16),
        ),
        in_specs=[IN_VMEM],
        out_specs=(IN_VMEM, IN_VMEM),
        compiler_params=PARAMS,
    )(back)


def close_kernel(core_ref, near_ref, far_ref, back_ref, images_ref, texts_ref, img_ref, txt_ref):
    first = core_ref[0] == 0
    q_sum = near_ref[...] + far_ref[...].astype(jnp.float32)
    p_sum = line_sum(back_ref, 0, near_ref.shape[0])
    img_ref[...] = raw_grad(jnp.where(first, p_sum, q_sum), images_ref[...])
    txt_ref[...] = raw_grad(jnp.where(first, q_sum, p_sum), texts_ref[...])


def close_rows(core, near, far, back, images, texts):
    shape = jax.ShapeDtypeStruct(near.shape, jnp.float32)
    return pl.pallas_call(
        close_kernel,
        out_shape=(shape, shape),
        in_specs=[IN_SMEM] + [IN_VMEM] * 5,
        out_specs=(IN_VMEM, IN_VMEM),
        compiler_params=PARAMS,
    )(core, near, far, back, images, texts)


def in_hbm(array):
    return pltpu.with_memory_space_constraint(array, pltpu.HBM)


def in_vmem(array):
    return pltpu.with_memory_space_constraint(array, pltpu.VMEM)


def trade(blocks, role, order):
    groups = line_groups(role, order)
    return lax.all_to_all(
        blocks, AXES, split_axis=0, concat_axis=0, axis_index_groups=groups, tiled=True
    )


def place_in(order, at):
    return sum(jnp.where(at == where, place, 0) for place, where in enumerate(order))


def swap_x(block, role):
    return lax.ppermute(block, AXES, across_x(role))


def p_role(core):
    return core


def q_role(core):
    return 1 - core


def local(images, texts):
    rows, width = images.shape
    bf = jnp.bfloat16
    core = lax.axis_index("core")
    y, z = lax.axis_index("y"), lax.axis_index("z")
    p_place = place_in(P_ORDER, jnp.where(core == 0, z, y))
    q_place = place_in(Q_ORDER, jnp.where(core == 0, y, z))
    core = core.astype(jnp.int32).reshape(1)

    copies_p, own_q = open_rows(core, in_hbm(images), in_hbm(texts))
    near_p = trade(copies_p, p_role, P_ORDER).reshape(-1, width)
    copies_q = copies(own_q, swap_x(own_q, q_role))
    near_p = hold(near_p, [in_hbm(copies_q)])
    mine_q = trade(copies_q, q_role, Q_ORDER)
    far_p = swap_x(near_p, p_role)
    theirs_p = in_hbm(lax.ppermute(jnp.concatenate([near_p, far_p], 0), "core", SWAP))

    at_pq = jnp.stack([p_place * rows, q_place * 2 * rows, rows]).astype(jnp.int32)
    at_qp = jnp.stack([q_place * 2 * rows, p_place * rows, rows]).astype(jnp.int32)
    all_q = [(mine_q, None)]
    theirs_q = in_vmem(lax.ppermute(mine_q.reshape(-1, width), "core", SWAP))
    sum_q = pull(all_q, [near_p, far_p], at=at_qp, labelled=(0, 0), after=theirs_p, dtype=bf)
    sum_q = pull(all_q, [theirs_q], so_far=sum_q, kind="line", dtype=bf)
    near, far = sum_rows(trade(sum_q.reshape(mine_q.shape), q_role, Q_ORDER))
    far = swap_x(far, q_role)

    others = [mine_q, theirs_p]
    back_p = swap_x(pull([(far_p, None)], others, load=True, dtype=bf), p_role)
    near_p = pull([(near_p, None)], others, at=at_pq, labelled=(0, 0), load=True)
    back_p = trade(add_rows(near_p, back_p), p_role, P_ORDER)
    return close_rows(core, near, far, back_p, images, texts)


def solution(mesh):
    fine = Mesh(mesh.devices.reshape(SIZES), AXES)
    return jax.shard_map(
        local, mesh=fine, in_specs=(ALL, ALL), out_specs=(ALL, ALL), check_vma=False
    )
```
